512 devices in a mesh: source: 8 (over y_hi, core), cand: 8 (over x, y_lo), tensor: 8 (over z).
Axes of the slice: x: 4, y: 8 (y_hi: 4, y_lo: 2; y = y_hi * 2 + y_lo), z: 8, core: 2. Of those that a mesh axis runs over, the one named last changes fastest.
Arguments:
- dec_states: bfloat16 [8, 8, 128, 4096], P('source', 'cand', None, 'tensor'), may hold values from -6 to 6
- enc_states: bfloat16 [8, 96, 4096], P('source', None, 'cand'), may hold values from -6 to 6
- norm_gain: float32 [4096], replicated, may hold values from 0.5 to 1.5
- w_query: bfloat16 [4096, 2048], P('cand', 'tensor'), may hold values from -0.09375 to 0.09375
- w_key: bfloat16 [4096, 2048], P('cand', 'tensor'), may hold values from -0.09375 to 0.09375
- w_value: bfloat16 [4096, 2048], P('cand', 'tensor'), may hold values from -0.09375 to 0.09375
- w_out: bfloat16 [2048, 4096], P('tensor', 'cand'), may hold values from -0.125 to 0.125
- target_rows: bfloat16 [8, 8, 128, 4096], P('source', 'cand'), may hold values from -6 to 6
- cand_lengths: int32 [8, 8], P('source', 'cand'), may hold values from 1 to 128, 640 in all within a row
- src_lengths: int32 [8], P('source'), may hold values from 1 to 96, 576 in all
- costs: int32 [8, 8], P('source', 'cand'), may hold values from 0 to 100
Outputs:
- loss: float32 [], replicated
- grad_dec: float32 [8, 8, 128, 4096], P('source', 'cand', None, 'tensor')
- grad_enc: float32 [8, 96, 4096], P('source', 'tensor', 'cand')
- radial_grad: float32 [8, 8, 128], P('source', 'cand')
The draws below stay inside these ranges and needn't reach their ends.
Inputs may be any that keep to these rules, and one draw needn't show every extreme that they name: `cand_lengths`: for each source the 8 lengths sum to 640 and the longest is exactly 128. `src_lengths`: the 8 lengths sum to 576 and the longest is exactly 96.
All inputs are finite; a program needn't handle non-finite values. No bound on the sum of `cand_lengths` or of `src_lengths` on one device may be relied on, other than what follows from the above.
Results may differ from the reference program's by a relative error of at most 0.033.
Values may be sent and summed in bfloat16 or wider, within the bound.
A program may use at most 64 MiB of HBM per device.

```python
import math
import jax
import jax.numpy as jnp
import numpy as np
from jax import lax

D = 4096
HEADS = 32
HEAD_DIM = 64
TGT = 128
SRC = 96
SOURCES = 8
CANDS = 8


def place_ends(drawn, stream_key, low, top_value):
    place = [jax.random.randint(jax.random.fold_in(stream_key, axis), (), 0, length) for axis, length in enumerate(drawn.shape)]
    main_axis = drawn.shape.index(max(drawn.shape))
    neighbour = place[:main_axis] + [(place[main_axis] + 1) % drawn.shape[main_axis]] + place[main_axis + 1:]
    return drawn.at[tuple(place)].set(low).at[tuple(neighbour)].set(top_value)


def level_of(stream_key, shape, shards, smallest, largest):
    level, own = 1.0, jax.random.fold_in(stream_key, 6)
    for dim, parts in shards:
        steps = jnp.exp(jax.random.uniform(jax.random.fold_in(own, dim), (parts,), jnp.float32, smallest / len(shards), largest / len(shards)))
        level = level * jnp.repeat(steps, shape[dim] // parts).reshape([-1 if axis == dim else 1 for axis in range(len(shape))])
    return level


def split_up(count, total, reach, slope):
    weights = [(1 << 20) // math.isqrt(standing ** slope) + 1 for standing in range(2, count + 1)]
    surplus, counts = total - reach - (count - 1), [1] * (count - 1)
    while surplus > 0:
        candidates = [i for i in range(count - 1) if counts[i] < reach]
        pool, budget = sum([weights[i] for i in candidates]), surplus
        for i in candidates:
            extra = min(reach - counts[i], max(1, budget * weights[i] // pool), surplus)
            counts[i] = counts[i] + extra
            surplus = surplus - extra
    return np.array([reach] + counts)


def ragged(stream_key, number_of, total, limit, skew):
    if number_of == 2:
        one = jax.random.randint(stream_key, (), max(1, total - limit), min(limit, total - 1) + 1)
        return jnp.stack([one, total - one])
    lengths = jnp.asarray(split_up(number_of, total, limit, skew), jnp.int32)
    pairs = (number_of - 1) // 2
    donor, taker = lengths[1:1 + 2 * pairs:2], lengths[2:2 + 2 * pairs:2]
    margin = jnp.minimum(donor - 1, limit - taker)
    passed = jax.random.randint(jax.random.fold_in(stream_key, 1), (pairs,), 0, 1 << 20) % (margin + 1)
    lengths = lengths.at[1:1 + 2 * pairs:2].set(donor - passed).at[2:2 + 2 * pairs:2].set(taker + passed)
    return lengths[jax.random.permutation(jax.random.fold_in(stream_key, 2), number_of)]


def centred(stream_key, dims, spread, bound, shards=(), held_as=jnp.bfloat16):
    factor_of = level_of(stream_key, dims, shards, -0.22, 0.18) if shards else 1.0
    values = jax.random.normal(stream_key, dims, jnp.float32) * spread * factor_of
    return jnp.minimum(jnp.maximum(values, -bound), bound).astype(held_as)


def setup_inputs(seed: int = 0) -> dict:
    seeds = jax.random.split(jax.random.key(seed), 12)
    dec_states = centred(seeds[0], (SOURCES, CANDS, TGT, D), 1.0, 6.0, ((0, 8), (1, 8), (3, 8)))
    enc_states = centred(seeds[1], (SOURCES, SRC, D), 1.0, 6.0, ((0, 8), (2, 8)))
    norm_gain = jnp.clip(1.0 + 0.1 * jax.random.normal(seeds[2], (D,), jnp.float32), 0.5, 1.5)
    w_query = centred(seeds[3], (D, HEADS * HEAD_DIM), D ** -0.5, 0.09375, ((0, 8), (1, 8)))
    w_key = centred(seeds[4], (D, HEADS * HEAD_DIM), D ** -0.5, 0.09375, ((0, 8), (1, 8)))
    w_value = centred(seeds[5], (D, HEADS * HEAD_DIM), D ** -0.5, 0.09375, ((0, 8), (1, 8)))
    w_out = centred(seeds[6], (HEADS * HEAD_DIM, D), (HEADS * HEAD_DIM) ** -0.5, 0.125, ((0, 8), (1, 8)))
    target_rows = centred(seeds[7], (SOURCES, CANDS, TGT, D), 1.0, 6.0, ((0, 8), (1, 8)))
    cand_lengths = jax.vmap(lambda own: ragged(own, CANDS, 5 * CANDS * TGT // 8, TGT, 1))(jax.random.split(seeds[8], SOURCES)).reshape((SOURCES, CANDS)).astype(jnp.int32)
    src_lengths = ragged(seeds[9], SOURCES, 3 * SOURCES * SRC // 4, SRC, 1).astype(jnp.int32)
    costs = place_ends(jax.random.randint(seeds[10], (SOURCES, CANDS), 0, 101), jax.random.fold_in(seeds[10], 1), 0, 100).astype(jnp.int32)
    return {"dec_states": dec_states, "enc_states": enc_states, "norm_gain": norm_gain, "w_query": w_query, "w_key": w_key, "w_value": w_value, "w_out": w_out, "target_rows": target_rows, "cand_lengths": cand_lengths, "src_lengths": src_lengths, "costs": costs}


def settle(value):
    return lax.optimization_barrier(value.astype(jnp.bfloat16)).astype(jnp.float32)

def reference(dec_states, enc_states, norm_gain, w_query, w_key, w_value, w_out, target_rows, cand_lengths, src_lengths, costs):
    width_all = HEADS * HEAD_DIM
    scale = HEAD_DIM ** (-0.5)
    x = dec_states.astype(jnp.float32)
    inv_rms = lax.rsqrt(lax.optimization_barrier(jnp.mean(x * x, axis=-1, keepdims=True)) + 1e-06)
    gain = norm_gain.astype(jnp.float32)
    normed = (x * inv_rms * gain).astype(jnp.bfloat16)
    query = jnp.dot(normed.reshape(-1, D), w_query, preferred_element_type=jnp.float32).astype(jnp.bfloat16)
    keys = jnp.dot(enc_states.reshape(-1, D), w_key, preferred_element_type=jnp.float32).astype(jnp.bfloat16)
    values = jnp.dot(enc_states.reshape(-1, D), w_value, preferred_element_type=jnp.float32).astype(jnp.bfloat16)
    q5 = query.astype(jnp.float32).reshape(SOURCES, CANDS, TGT, HEADS, HEAD_DIM)
    k4 = keys.astype(jnp.float32).reshape(SOURCES, SRC, HEADS, HEAD_DIM)
    v4 = values.astype(jnp.float32).reshape(SOURCES, SRC, HEADS, HEAD_DIM)
    logits = jnp.einsum('scthd,sjhd->schtj', q5, k4) * scale
    key_mask = (jnp.arange(SRC)[None, :] < src_lengths[:, None]).astype(jnp.float32)
    expo = jnp.exp(logits) * key_mask[:, None, None, None, :]
    probs_f = expo / lax.optimization_barrier(jnp.sum(expo, axis=-1, keepdims=True))
    probs = settle(probs_f)
    context = jnp.einsum('schtj,sjhd->scthd', probs, v4).astype(jnp.bfloat16).reshape(-1, width_all)
    term = jnp.dot(context, w_out, preferred_element_type=jnp.float32).reshape(SOURCES, CANDS, TGT, D)
    out = x + term
    tok_mask = (jnp.arange(TGT)[None, None, :] < cand_lengths[:, :, None]).astype(jnp.float32)
    factor = tok_mask / jnp.sqrt(D * cand_lengths.astype(jnp.float32))[:, :, None]
    rows = target_rows.astype(jnp.float32)
    score = lax.optimization_barrier(jnp.sum(lax.optimization_barrier(jnp.sum(out * rows, axis=-1)) * factor, axis=-1))
    weight = jnp.exp(score)
    risk = costs.astype(jnp.float32) / 100.0
    total = lax.optimization_barrier(jnp.sum(weight, axis=1, keepdims=True))
    expected = lax.optimization_barrier(jnp.sum(weight * risk, axis=1, keepdims=True)) / total
    loss = jnp.sum(expected) / SOURCES
    pbar = weight / total
    grad_score = pbar * (risk - expected) / SOURCES
    grad_out = ((grad_score[:, :, None] * factor)[..., None] * rows).astype(jnp.bfloat16)
    grad_ctx = jnp.dot(grad_out.reshape(-1, D), w_out.T, preferred_element_type=jnp.float32).astype(jnp.bfloat16)
    gc5 = grad_ctx.astype(jnp.float32).reshape(SOURCES, CANDS, TGT, HEADS, HEAD_DIM)
    grad_probs = jnp.einsum('scthd,sjhd->schtj', gc5, v4)
    grad_logits = settle(probs_f * (grad_probs - lax.optimization_barrier(jnp.sum(probs_f * grad_probs, axis=-1, keepdims=True))) * scale)
    grad_query = jnp.einsum('schtj,sjhd->scthd', grad_logits, k4).astype(jnp.bfloat16)
    grad_key = jnp.einsum('schtj,scthd->scjhd', grad_logits, q5).astype(jnp.bfloat16)
    grad_value = jnp.einsum('schtj,scthd->scjhd', probs, gc5).astype(jnp.bfloat16)
    key_sum = lax.optimization_barrier(jnp.sum(grad_key.astype(jnp.float32), axis=1)).reshape(-1, width_all)
    value_sum = lax.optimization_barrier(jnp.sum(grad_value.astype(jnp.float32), axis=1)).reshape(-1, width_all)
    grad_enc = jnp.dot(key_sum, w_key.astype(jnp.float32).T, precision=lax.Precision.HIGHEST)
    grad_enc = grad_enc + jnp.dot(value_sum, w_value.astype(jnp.float32).T, precision=lax.Precision.HIGHEST)
    grad_normed = jnp.dot(grad_query.reshape(-1, width_all), w_query.T, preferred_element_type=jnp.float32).reshape(SOURCES, CANDS, TGT, D)
    inner = lax.optimization_barrier(jnp.sum(gain * grad_normed * x, axis=-1, keepdims=True))
    grad_dec = grad_out.astype(jnp.float32) + inv_rms * gain * grad_normed - x * inv_rms ** 3 * inner / D
    radial_grad = inner[..., 0] / jnp.sqrt(jnp.float32(D))
    return (loss, grad_dec, grad_enc.reshape(SOURCES, SRC, D), radial_grad)
```

```python
import jax
import jax.numpy as jnp
from jax import lax
from jax.experimental import pallas as pl
from jax.experimental.pallas import tpu as pltpu
from jax.sharding import PartitionSpec as P

HEAD_DIM = 64
N = 8
XS = 4
CH = 4
MESH = pl.DeviceIdType.MESH
BF = jnp.bfloat16
F32 = jnp.float32


def dot(left, right):
    return jnp.dot(left, right, preferred_element_type=F32)


def dot_tt(left, right):
    return lax.dot_general(left, right, (((1,), (1,)), ((), ())), preferred_element_type=F32)


def dot_00(left, right):
    return lax.dot_general(left, right, (((0,), (0,)), ((), ())), preferred_element_type=F32)


def hop_exists(way, hop, chunk):
    return hop <= 3 or (hop == 4 and (chunk < CH // 2) == (way == 0))


def kernel(
    x_ref, enc_ref, gain_ref, wq_ref, wk_ref, wv_ref, wo_ref, rows_ref, clen_ref, slen_ref, cost_ref,
    loss_ref, gdec_ref, genc_ref, rad_ref,
    xg, wqf, wof, kvs, kvr, kvo, kvf, dks, dkr, dko, zt, ct, lt, ens, enr, rso, rsr, own,
    xss, xsr, wxs, wxr, wys, wyr, wss, wsr, k1s, k1r, k2s, k2r, d1s, d1r, d2s, d2r,
    zss, zsr, css, csr, lss, lsr, ess, esr, rss, rsrs,
):
    s, c, z = lax.axis_index("source"), lax.axis_index("cand"), lax.axis_index("tensor")
    core, xx, yl = lax.rem(s, 2), c // 2, lax.rem(c, 2)
    sgn = 1 - 2 * core
    tgt, wide = x_ref.shape
    width = wide * N
    cols = wq_ref.shape[1]
    srcs = enc_ref.shape[0]
    pad = kvf.shape[0]
    group = srcs // N
    gpad = pad // N

    def up(i, k):
        return lax.rem(i + k + N, N)

    def remote(src, dst, ssem, rsem, dev):
        return pltpu.make_async_remote_copy(
            src_ref=src, dst_ref=dst, send_sem=ssem, recv_sem=rsem, device_id=dev, device_id_type=MESH
        )

    y_to = {"source": up(s, 2 * yl * (1 - core) - 2 * (1 - yl) * core), "cand": c + 1 - 2 * yl}
    y_from = {"source": up(s, 2 * yl * core - 2 * (1 - yl) * (1 - core)), "cand": c + 1 - 2 * yl}

    barrier = pltpu.get_barrier_semaphore()
    for k in range(1, N):
        pl.semaphore_signal(barrier, inc=1, device_id={"tensor": up(z, k)}, device_id_type=MESH)
        pl.semaphore_signal(barrier, inc=1, device_id={"cand": up(c, k)}, device_id_type=MESH)
        pl.semaphore_signal(barrier, inc=1, device_id={"source": up(s, k)}, device_id_type=MESH)
    pl.semaphore_signal(barrier, inc=1, device_id=y_from, device_id_type=MESH)
    pl.semaphore_wait(barrier, 3 * (N - 1) + 1)

    started = []

    def go(copy):
        copy.start()
        started.append(copy)

    step = tgt // CH

    def x_copy(way, hop, chunk):
        to = 1 if way == 0 else -1
        block = up(z, -to * (hop - 1))
        part = pl.ds(chunk * step, step)
        src = x_ref.at[part] if hop == 1 else xg.at[block, part]
        return remote(src, xg.at[block, part], xss.at[way, hop - 1, chunk], xsr.at[way, hop - 1, chunk], {"tensor": up(z, to)})

    def x_round(hop):
        for chunk in range(CH):
            for way in range(2):
                if hop_exists(way, hop, chunk):
                    x_copy(way, hop, chunk).wait_recv()
                    if hop_exists(way, hop + 1, chunk):
                        go(x_copy(way, hop + 1, chunk))

    hq, ho = wq_ref.shape[0] // 2, wo_ref.shape[0] // 2
    half = (pl.ds(pl.multiple_of(core * hq, hq), hq), pl.ds(pl.multiple_of(core * ho, ho), ho))
    full = (wqf, wof)
    mine = (wq_ref, wo_ref)

    def piece(dx, dy):
        return lax.rem(xx + dx + XS, XS) * 2 + (yl if dy == 0 else 1 - yl)

    def x_dev(to):
        return {"cand": lax.rem(xx + to + XS, XS) * 2 + yl}

    def w_own(m, i):
        return remote(mine[m].at[half[m]], full[m].at[c, half[m]], wxs.at[m, i], wxr.at[m, i], x_dev(1 - 2 * i))

    def w_relay(m):
        there = full[m].at[piece(-sgn, 0), half[m]]
        return remote(there, there, wxs.at[m, 2], wxr.at[m, 2], x_dev(sgn))

    def w_x_wait(m, i):
        remote(mine[m].at[half[m]], full[m].at[c, half[m]], wxs.at[m, i], wxr.at[m, i], x_dev(1)).wait_recv()

    hops = (0, -sgn, sgn, 2)

    def w_y(m, i):
        dst = full[m].at[piece(hops[i], 0), half[m]]
        src = mine[m].at[half[m]] if i == 0 else dst
        return remote(src, dst, wys.at[m, i], wyr.at[m, i], y_to)

    def w_sib(m, i):
        there = full[m].at[piece(hops[i % 4], i // 4), half[m]]
        return remote(there, there, wss.at[m, i - 1], wsr.at[m, i - 1], {"source": s + sgn})

    def w_first(m):
        w_x_wait(m, core)
        go(w_relay(m))
        go(w_y(m, 1))
        go(w_sib(m, 1))
        w_x_wait(m, 1 - core)
        go(w_y(m, 2))
        go(w_sib(m, 2))
        w_y(m, 0).wait_recv()
        go(w_sib(m, 4))

    def w_second(m):
        w_relay(m).wait_recv()
        go(w_y(m, 3))
        go(w_sib(m, 3))
        for i in (1, 2):
            w_y(m, i).wait_recv()
            go(w_sib(m, 4 + i))

    def w_third(m):
        w_y(m, 3).wait_recv()
        go(w_sib(m, 7))

    def w_last(m):
        for i in range(1, N):
            w_sib(m, i).wait_recv()

    for chunk in range(CH):
        for way in range(2):
            go(x_copy(way, 1, chunk))
    for i in range(2):
        go(w_own(0, i))
    go(w_y(0, 0))

    row = lax.broadcasted_iota(jnp.int32, (pad, srcs), 0)
    col = lax.broadcasted_iota(jnp.int32, (pad, srcs), 1)
    spot = lax.rem(row, gpad)
    spread = jnp.where((spot < group) & (row // gpad * group + spot == col), 1.0, 0.0).astype(BF)
    enc = dot(spread, enc_ref[...]).astype(BF)
    k_part = dot(enc, wk_ref[...])
    v_part = dot(enc, wv_ref[...])

    def put_blocks(dst, left, right):
        for g in range(4):
            src = (left if g < 2 else right)[:, (g % 2) * 128 : (g % 2) * 128 + 128].astype(BF)
            for r in range(2):
                dst[g * 2 + r] = src[r * (pad // 2) : (r + 1) * (pad // 2)]

    def cand_all(send_of, dst, ssem, rsem, k):
        return remote(send_of(up(c, k)), dst.at[c], ssem.at[k], rsem.at[k], {"cand": up(c, k)})

    put_blocks(kvs, k_part, v_part)

    def kv1(k):
        return cand_all(lambda i: kvs.at[i], kvr, k1s, k1r, k)

    def kv2(k):
        return cand_all(lambda i: kvo.at[c], kvo, k2s, k2r, k)

    for k in range(1, N):
        go(kv1(k))
    for i in range(2):
        go(w_own(1, i))
    go(w_y(1, 0))

    xg[z] = x_ref[...]
    wqf[c] = wq_ref[...]
    wof[c] = wo_ref[...]

    x_round(1)
    w_first(0)
    x_round(2)
    kvr[c] = kvs[c]
    for k in range(1, N):
        kv1(k).wait_recv()
    total = kvr[0].astype(F32)
    for i in range(1, N):
        total = total + kvr[i].astype(F32)
    kvo[c] = total.astype(BF)
    for k in range(1, N):
        go(kv2(k))
    w_second(0)
    w_first(1)
    x_round(3)
    w_third(0)
    w_second(1)
    x_round(4)
    w_third(1)

    for k in range(1, N):
        kv2(k).wait_recv()
    for g in range(4):
        for r in range(2):
            kvf[r * (pad // 2) : (r + 1) * (pad // 2), g * 128 : (g + 1) * 128] = kvo[g * 2 + r]

    w_last(0)

    def q_step(b, carry):
        acc, squares = carry
        block = xg[b].astype(F32)
        gained = (block * gain_ref[:, pl.ds(pl.multiple_of(b * wide, wide), wide)]).astype(BF)
        return acc + dot(gained, wqf[b]), squares + jnp.sum(block * block, axis=1, keepdims=True)

    q_raw, squares = lax.fori_loop(0, N, q_step, (jnp.zeros((tgt, cols), F32), jnp.zeros((tgt, 1), F32)))
    mean = squares / width + 1e-06
    inv_rms = lax.rsqrt(mean)
    query = (q_raw * inv_rms).astype(BF)

    w_last(1)

    def r_step(b, acc):
        return acc + dot_tt(rows_ref[:, pl.ds(pl.multiple_of(b * wide, wide), wide)], wof[b])

    back = lax.fori_loop(0, N, r_step, jnp.zeros((tgt, cols), F32))
    back_b = back.astype(BF)

    length = jnp.full((tgt, 1), clen_ref[0, 0], jnp.int32)
    inside = (lax.broadcasted_iota(jnp.int32, (tgt, 1), 0) < length).astype(F32)
    factor = inside / jnp.sqrt(width * length.astype(F32))
    place = lax.broadcasted_iota(jnp.int32, (1, pad), 1)
    spot = lax.rem(place, gpad)
    real = (spot < group) & (place // gpad * group + spot < jnp.full((1, pad), slen_ref[0], jnp.int32))
    key_mask = real.astype(F32)
    scale = HEAD_DIM ** (-0.5)
    scaled_back = (back * factor).astype(BF)

    x_part = x_ref[...].astype(F32)
    rows_part = rows_ref[:, pl.ds(pl.multiple_of(z * wide, wide), wide)].astype(F32)
    dots = jnp.sum(x_part * rows_part, axis=1, keepdims=True)
    d_query, d_key, d_value = [], [], []
    for h in range(cols // HEAD_DIM):
        at = slice(h * HEAD_DIM, (h + 1) * HEAD_DIM)
        keys = kvf[:, at]
        values = kvf[:, cols + h * HEAD_DIM : cols + (h + 1) * HEAD_DIM]
        expo = jnp.exp(dot_tt(query[:, at], keys) * scale) * key_mask
        probs = expo / jnp.sum(expo, axis=1, keepdims=True)
        reach = dot_tt(back_b[:, at], values)
        along = jnp.sum(probs * reach, axis=1, keepdims=True)
        dots = dots + along
        d_logits = (probs * (reach - along) * (scale * factor)).astype(BF)
        d_query.append(dot(d_logits, keys))
        d_key.append(dot_00(d_logits, query[:, at]))
        d_value.append(dot_00(probs.astype(BF), scaled_back[:, at]))
    d_query = jnp.concatenate(d_query, axis=1)
    put_blocks(dks, jnp.concatenate(d_key, axis=1), jnp.concatenate(d_value, axis=1))

    eye = lax.broadcasted_iota(jnp.int32, (tgt, tgt), 0) == lax.broadcasted_iota(jnp.int32, (tgt, tgt), 1)
    inner_part = jnp.sum(
        jnp.where(eye, jnp.sum(d_query * q_raw, axis=1, keepdims=True), 0.0), axis=0, keepdims=True
    )
    score_part = jnp.sum(dots * factor, axis=0, keepdims=True)
    line = lax.broadcasted_iota(jnp.int32, (8, 128), 0)
    zt[z] = jnp.where(line == 0, score_part, jnp.where(line == 1, inner_part, 0.0))

    def z_tile(k):
        return remote(zt.at[z], zt.at[z], zss.at[k], zsr.at[k], {"tensor": up(z, k)})

    def c_tile(k):
        return remote(ct.at[c], ct.at[c], css.at[k], csr.at[k], {"cand": up(c, k)})

    def l_tile(k):
        return remote(lt.at[s], lt.at[s], lss.at[k], lsr.at[k], {"source": up(s, k)})

    def dk1(k):
        return cand_all(lambda i: dks.at[i], dkr, d1s, d1r, k)

    def dk2(k):
        return cand_all(lambda i: dko.at[c], dko, d2s, d2r, k)

    def en(k):
        return remote(ens.at[up(z, k)], enr.at[z], ess.at[k], esr.at[k], {"tensor": up(z, k)})

    for k in range(1, N):
        go(z_tile(k))
    for k in range(1, N):
        go(dk1(k))

    dq = d_query.astype(BF)

    def term(dest):
        return dot_tt(dq, wqf[dest])

    def rs_copy(way, hop, chunk):
        part = pl.ds(chunk * step, step)
        return remote(
            rso.at[way, hop - 1, part], rsr.at[way, hop - 1, part],
            rss.at[way, hop - 1, chunk], rsrs.at[way, hop - 1, chunk], {"tensor": up(z, 1 if way == 0 else -1)},
        )

    def rs_round(hop):
        for way in range(2):
            own[way] = term(up(z, hop if way == 0 else -hop))
        fresh = [(w, ch) for w in range(2) for ch in range(CH) if not hop_exists(w, hop + 1, ch)]
        late = [(w, ch) for ch in range(CH) for w in range(2) if hop_exists(w, hop + 1, ch)]
        for way, chunk in fresh + late:
            if not hop_exists(way, hop, chunk):
                continue
            part = pl.ds(chunk * step, step)
            value = own[way, part]
            if hop_exists(way, hop + 1, chunk):
                rs_copy(way, hop + 1, chunk).wait_recv()
                value = value + rsr[way, hop, part].astype(F32)
            rso[way, hop - 1, part] = value.astype(BF)
            go(rs_copy(way, hop, chunk))

    rs_round(4)

    for k in range(1, N):
        z_tile(k).wait_recv()
    sums = zt[0]
    for i in range(1, N):
        sums = sums + zt[i]
    weight = jnp.exp(sums[0:1])
    inner = sums[1:2]
    risk = jnp.full((1, 128), cost_ref[0, 0], jnp.int32).astype(F32) / 100.0
    ct[c] = jnp.where(line == 0, weight, jnp.where(line == 1, risk, 0.0))
    for k in range(1, N):
        go(c_tile(k))

    rs_round(3)

    for k in range(1, N):
        c_tile(k).wait_recv()
    total_w, total_wr = ct[0, 0:1], ct[0, 0:1] * ct[0, 1:2]
    for i in range(1, N):
        total_w = total_w + ct[i, 0:1]
        total_wr = total_wr + ct[i, 0:1] * ct[i, 1:2]
    expected = total_wr / total_w
    lt[s] = jnp.broadcast_to(expected, (8, 128))
    for k in range(1, N):
        go(l_tile(k))
    dkr[c] = dks[c]
    for k in range(1, N):
        dk1(k).wait_recv()
    total = jnp.zeros(dkr.shape[1:], F32)
    for i in range(N):
        share = ct[i, 0:1] / total_w * (ct[i, 1:2] - expected) / N
        total = total + share * dkr[i].astype(F32)
    dko[c] = total.astype(BF)
    for k in range(1, N):
        go(dk2(k))

    rs_round(2)

    for k in range(1, N):
        dk2(k).wait_recv()
    sides = []
    for g in range(4):
        sides.append(jnp.concatenate([dko[g * 2], dko[g * 2 + 1]], axis=0))
    enc_term = dot_tt(jnp.concatenate(sides[:2], axis=1), wk_ref[...])
    enc_term = enc_term + dot_tt(jnp.concatenate(sides[2:], axis=1), wv_ref[...])
    for i in range(N):
        ens[i] = enc_term[i * gpad : (i + 1) * gpad].astype(BF)
    for k in range(1, N):
        go(en(k))

    rs_round(1)

    enr[z] = ens[z]
    for k in range(1, N):
        en(k).wait_recv()
    total = enr[0].astype(F32)
    for i in range(1, N):
        total = total + enr[i].astype(F32)
    genc_ref[...] = total[:group]

    for k in range(1, N):
        l_tile(k).wait_recv()
    loss = lt[0, 0:1]
    for i in range(1, N):
        loss = loss + lt[i, 0:1]
    loss_ref[...] = loss / N

    share = weight / total_w * (risk - expected) / N
    rad_ref[...] = share * inner / jnp.sqrt(jnp.full((1, 128), width, F32))
    share_col = share[:, 0:1]
    inner_col = jnp.sum(jnp.where(eye, inner, 0.0), axis=1, keepdims=True)
    own[0] = term(z)
    for chunk in range(CH):
        for way in range(2):
            rs_copy(way, 1, chunk).wait_recv()
    normed_grad = own[0] + rsr[0, 0].astype(F32) + rsr[1, 0].astype(F32)
    gain_part = gain_ref[:, pl.ds(pl.multiple_of(z * wide, wide), wide)]
    gdec_ref[...] = share_col * (
        factor * rows_part
        + inv_rms * gain_part * normed_grad
        - x_part * (inv_rms * inv_rms * inv_rms * inner_col / width)
    )
    for copy in started:
        copy.wait_send()


def local(
    dec_states, enc_states, norm_gain, w_query, w_key, w_value, w_out, target_rows, cand_lengths, src_lengths, costs
):
    x = dec_states[0, 0]
    enc = enc_states[0]
    tgt, wide = x.shape
    srcs = enc.shape[0]
    depth, cols = w_query.shape
    group = srcs // N
    gpad = -(-group // 16) * 16
    pad = gpad * N
    vmem = pl.BlockSpec(memory_space=pltpu.VMEM)
    smem = pl.BlockSpec(memory_space=pltpu.SMEM)
    dma = pltpu.SemaphoreType.DMA
    block = (N, pad // 2, 128)
    loss, grad_dec, grad_enc, radial = pl.pallas_call(
        kernel,
        out_shape=(
            jax.ShapeDtypeStruct((1, 128), F32),
            jax.ShapeDtypeStruct((tgt, wide), F32),
            jax.ShapeDtypeStruct((group, depth), F32),
            jax.ShapeDtypeStruct((1, tgt), F32),
        ),
        in_specs=[vmem] * 8 + [smem] * 3,
        out_specs=(vmem,) * 4,
        scratch_shapes=[
            pltpu.VMEM((N, tgt, wide), BF),
            pltpu.VMEM((N, depth, cols), BF),
            pltpu.VMEM((N, cols, depth), BF),
            pltpu.VMEM(block, BF),
            pltpu.VMEM(block, BF),
            pltpu.VMEM(block, BF),
            pltpu.VMEM((pad, 2 * cols), BF),
            pltpu.VMEM(block, BF),
            pltpu.VMEM(block, BF),
            pltpu.VMEM(block, BF),
            pltpu.VMEM((N, 8, 128), F32),
            pltpu.VMEM((N, 8, 128), F32),
            pltpu.VMEM((N, 8, 128), F32),
            pltpu.VMEM((N, gpad, depth), BF),
            pltpu.VMEM((N, gpad, depth), BF),
            pltpu.VMEM((2, 4, tgt, wide), BF),
            pltpu.VMEM((2, 4, tgt, wide), BF),
            pltpu.VMEM((2, tgt, wide), F32),
            dma((2, 4, CH)), dma((2, 4, CH)),
            dma((2, 3)), dma((2, 3)),
            dma((2, 4)), dma((2, 4)),
            dma((2, 7)), dma((2, 7)),
        ]
        + [dma((N,))] * 16
        + [dma((2, 4, CH)), dma((2, 4, CH))],
        compiler_params=pltpu.CompilerParams(
            collective_id=0, has_side_effects=True, vmem_limit_bytes=48 * 1024 * 1024
        ),
    )(
        x, enc, norm_gain.reshape(1, -1), w_query, w_key, w_value, w_out, target_rows[0, 0],
        cand_lengths, src_lengths, costs,
    )
    return loss[0, 0], grad_dec[None, None], grad_enc[None], radial[None]


def solution(mesh):
    placed = (
        P("source", "cand", None, "tensor"),
        P("source", None, "cand"),
        P(),
        P("cand", "tensor"),
        P("cand", "tensor"),
        P("cand", "tensor"),
        P("tensor", "cand"),
        P("source", "cand", None, None),
        P("source", "cand"),
        P("source"),
        P("source", "cand"),
    )
    return jax.shard_map(
        local,
        mesh=mesh,
        in_specs=placed,
        out_specs=(
            P(),
            P("source", "cand", None, "tensor"),
            P("source", "tensor", "cand"),
            P("source", "cand", None),
        ),
        check_vma=False,
    )
```

```python
import jax
import jax.numpy as jnp
from jax import lax
from jax.experimental import pallas as pl
from jax.experimental.pallas import tpu as pltpu
from jax.sharding import PartitionSpec as P

HEAD_DIM = 64
N = 8
XS = 4
CH = 2
MESH = pl.DeviceIdType.MESH
BF = jnp.bfloat16
F32 = jnp.float32


def dot(left, right):
    return jnp.dot(left, right, preferred_element_type=F32)


def dot_tt(left, right):
    return lax.dot_general(left, right, (((1,), (1,)), ((), ())), preferred_element_type=F32)


def dot_00(left, right):
    return lax.dot_general(left, right, (((0,), (0,)), ((), ())), preferred_element_type=F32)


def hop_exists(way, hop, chunk):
    return hop <= 3 or (hop == 4 and (chunk < CH // 2) == (way == 0))


def kernel(
    x_in, enc_in, gain_in, wq_in, wk_in, wv_in, wo_in, rows_in, clen_ref, slen_ref, cost_ref,
    loss_ref, gdec_ref, genc_ref, rad_ref,
    enc_ref, gain_ref, wk_ref, wv_ref, rows_ref, loads, xn, xg, wqf, wof, kvs, kvr, kvo, kvf, dks, dkr, dko, zt, ct, lt, ens, enr, rso, rsr, own,
    xss, xsr, wxs, wxr, wys, wyr, wss, wsr, k1s, k1r, k2s, k2r, d1s, d1r, d2s, d2r,
    zss, zsr, css, csr, lss, lsr, ess, esr, rss, rsrs,
):
    s, c, z = lax.axis_index("source"), lax.axis_index("cand"), lax.axis_index("tensor")
    core, xx, yl = lax.rem(s, 2), c // 2, lax.rem(c, 2)
    sgn = 1 - 2 * core
    tgt, wide = x_in.shape
    width = wide * N
    cols = wq_in.shape[1]
    srcs = enc_ref.shape[0]
    pad = kvf.shape[0]
    group = srcs // N
    gpad = pad // N

    def up(i, k):
        return lax.rem(i + k + N, N)

    def remote(src, dst, ssem, rsem, dev):
        return pltpu.make_async_remote_copy(
            src_ref=src, dst_ref=dst, send_sem=ssem, recv_sem=rsem, device_id=dev, device_id_type=MESH
        )

    y_to = {"source": up(s, 2 * yl * (1 - core) - 2 * (1 - yl) * core), "cand": c + 1 - 2 * yl}
    y_from = {"source": up(s, 2 * yl * core - 2 * (1 - yl) * (1 - core)), "cand": c + 1 - 2 * yl}

    x_own, wq_own, wo_own = xg.at[z], wqf.at[c], wof.at[c]
    into = (x_own, wq_own, enc_ref, wk_ref, wv_ref, wo_own, rows_ref, gain_ref)
    local_copies = [
        pltpu.make_async_copy(src, dst, loads.at[i])
        for i, (src, dst) in enumerate(zip((x_in, wq_in, enc_in, wk_in, wv_in, wo_in, rows_in, gain_in), into))
    ]
    for copy in local_copies:
        copy.start()
    x_load, wq_load, enc_load, wk_load, wv_load, wo_load, rows_load, gain_load = local_copies

    barrier = pltpu.get_barrier_semaphore()
    for k in range(1, N):
        pl.semaphore_signal(barrier, inc=1, device_id={"tensor": up(z, k)}, device_id_type=MESH)
        pl.semaphore_signal(barrier, inc=1, device_id={"cand": up(c, k)}, device_id_type=MESH)
        pl.semaphore_signal(barrier, inc=1, device_id={"source": up(s, k)}, device_id_type=MESH)
    pl.semaphore_signal(barrier, inc=1, device_id=y_from, device_id_type=MESH)
    pl.semaphore_wait(barrier, 3 * (N - 1) + 1)

    started = []

    def go(copy):
        copy.start()
        started.append(copy)

    step = tgt // CH

    def x_copy(way, hop, chunk):
        to = 1 if way == 0 else -1
        block = up(z, -to * (hop - 1))
        part = pl.ds(chunk * step, step)
        return remote(xg.at[block, part], xg.at[block, part], xss.at[way, hop - 1, chunk], xsr.at[way, hop - 1, chunk], {"tensor": up(z, to)})

    def x_round(hop):
        for chunk in range(CH):
            for way in range(2):
                if hop_exists(way, hop, chunk):
                    x_copy(way, hop, chunk).wait_recv()
                    if hop_exists(way, hop + 1, chunk):
                        go(x_copy(way, hop + 1, chunk))

    hq, ho = wq_in.shape[0] // 2, wo_in.shape[0] // 2
    half = (pl.ds(pl.multiple_of(core * hq, hq), hq), pl.ds(pl.multiple_of(core * ho, ho), ho))
    full = (wqf, wof)

    def piece(dx, dy):
        return lax.rem(xx + dx + XS, XS) * 2 + (yl if dy == 0 else 1 - yl)

    def x_dev(to):
        return {"cand": lax.rem(xx + to + XS, XS) * 2 + yl}

    def w_own(m, i):
        there = full[m].at[c, half[m]]
        return remote(there, there, wxs.at[m, i], wxr.at[m, i], x_dev(1 - 2 * i))

    def w_relay(m):
        there = full[m].at[piece(-sgn, 0), half[m]]
        return remote(there, there, wxs.at[m, 2], wxr.at[m, 2], x_dev(sgn))

    def w_x_wait(m, i):
        there = full[m].at[c, half[m]]
        remote(there, there, wxs.at[m, i], wxr.at[m, i], x_dev(1)).wait_recv()

    hops = (0, -sgn, sgn, 2)

    def w_y(m, i):
        there = full[m].at[piece(hops[i], 0), half[m]]
        return remote(there, there, wys.at[m, i], wyr.at[m, i], y_to)

    def w_sib(m, i):
        there = full[m].at[piece(hops[i % 4], i // 4), half[m]]
        return remote(there, there, wss.at[m, i - 1], wsr.at[m, i - 1], {"source": s + sgn})

    def w_near(m):
        w_x_wait(m, core)
        go(w_relay(m))
        go(w_y(m, 1))
        go(w_sib(m, 1))
        w_x_wait(m, 1 - core)
        go(w_y(m, 2))
        go(w_sib(m, 2))

    def w_across(m):
        w_y(m, 0).wait_recv()
        go(w_sib(m, 4))

    def w_far(m):
        w_relay(m).wait_recv()
        go(w_y(m, 3))
        go(w_sib(m, 3))

    def w_corner(m):
        for i in (1, 2):
            w_y(m, i).wait_recv()
            go(w_sib(m, 4 + i))

    def w_end(m):
        w_y(m, 3).wait_recv()
        go(w_sib(m, 7))

    def w_got(m, i):
        w_sib(m, i).wait_recv()

    x_load.wait()
    for chunk in range(CH):
        for way in range(2):
            go(x_copy(way, 1, chunk))
    wq_load.wait()
    for i in range(2):
        go(w_own(0, i))
    go(w_y(0, 0))
    wo_load.wait()
    for i in range(2):
        go(w_own(1, i))
    go(w_y(1, 0))

    row = lax.broadcasted_iota(jnp.int32, (pad, srcs), 0)
    col = lax.broadcasted_iota(jnp.int32, (pad, srcs), 1)
    spot = lax.rem(row, gpad)
    spread = jnp.where((spot < group) & (row // gpad * group + spot == col), 1.0, 0.0).astype(BF)
    enc_load.wait()
    wk_load.wait()
    wv_load.wait()
    enc = dot(spread, enc_ref[...]).astype(BF)
    k_part = dot(enc, wk_ref[...])
    v_part = dot(enc, wv_ref[...])

    def put_blocks(dst, left, right):
        for g in range(4):
            src = (left if g < 2 else right)[:, (g % 2) * 128 : (g % 2) * 128 + 128].astype(BF)
            for r in range(2):
                dst[g * 2 + r] = src[r * (pad // 2) : (r + 1) * (pad // 2)]

    def cand_all(send_of, dst, ssem, rsem, k):
        return remote(send_of(up(c, k)), dst.at[c], ssem.at[k], rsem.at[k], {"cand": up(c, k)})

    put_blocks(kvs, k_part, v_part)

    def kv1(k):
        return cand_all(lambda i: kvs.at[i], kvr, k1s, k1r, k)

    def kv2(k):
        return cand_all(lambda i: kvo.at[c], kvo, k2s, k2r, k)

    for k in range(1, N):
        go(kv1(k))
    gain_load.wait()
    rows_load.wait()

    def gained(b):
        block = xg[b].astype(F32)
        xn[:, pl.ds(pl.multiple_of(b * wide, wide), wide)] = (
            block * gain_ref[:, pl.ds(pl.multiple_of(b * wide, wide), wide)]
        ).astype(BF)
        return jnp.sum(block * block, axis=1, keepdims=True)

    def r_term(b):
        return dot_tt(rows_ref[:, pl.ds(pl.multiple_of(b * wide, wide), wide)], wof[b])

    squares = gained(z)
    back = r_term(c)
    w_across(0)
    x_round(1)
    w_near(0)
    w_across(1)
    squares = squares + gained(up(z, 1)) + gained(up(z, -1))
    kvr[c] = kvs[c]
    for k in range(1, N):
        kv1(k).wait_recv()
    total = kvr[0].astype(F32)
    for i in range(1, N):
        total = total + kvr[i].astype(F32)
    kvo[c] = total.astype(BF)
    for k in range(1, N):
        go(kv2(k))
    x_round(2)
    w_near(1)
    w_far(0)
    squares = squares + gained(up(z, 2)) + gained(up(z, -2))
    w_corner(0)
    w_far(1)
    x_round(3)
    squares = squares + gained(up(z, 3)) + gained(up(z, -3))
    w_got(1, 4)
    back = back + r_term(piece(0, 1))
    w_got(1, 1)
    w_got(1, 2)
    back = back + r_term(piece(1, 0)) + r_term(piece(-1, 0))
    w_corner(1)
    w_end(0)
    x_round(4)
    squares = squares + gained(up(z, 4))
    w_got(1, 3)
    back = back + r_term(piece(2, 0))
    for k in range(1, N):
        kv2(k).wait_recv()
    for g in range(4):
        for r in range(2):
            kvf[r * (pad // 2) : (r + 1) * (pad // 2), g * 128 : (g + 1) * 128] = kvo[g * 2 + r]
    w_end(1)
    for i in range(1, N):
        w_got(0, i)
    q_raw = jnp.zeros((tgt, cols), F32)
    for b in range(N):
        q_raw = q_raw + dot(xn[:, b * wide : (b + 1) * wide], wqf[b])
    inv_rms = lax.rsqrt(squares / width + 1e-06)
    query = (q_raw * inv_rms).astype(BF)
    w_got(1, 5)
    w_got(1, 6)
    back = back + r_term(piece(1, 1)) + r_term(piece(-1, 1))
    w_got(1, 7)
    back = back + r_term(piece(2, 1))
    back_b = back.astype(BF)

    length = jnp.full((tgt, 1), clen_ref[0, 0], jnp.int32)
    inside = (lax.broadcasted_iota(jnp.int32, (tgt, 1), 0) < length).astype(F32)
    factor = inside / jnp.sqrt(width * length.astype(F32))
    place = lax.broadcasted_iota(jnp.int32, (1, pad), 1)
    spot = lax.rem(place, gpad)
    real = (spot < group) & (place // gpad * group + spot < jnp.full((1, pad), slen_ref[0], jnp.int32))
    key_mask = real.astype(F32)
    scale = HEAD_DIM ** (-0.5)
    scaled_back = (back * factor).astype(BF)

    x_part = xg[z].astype(F32)
    rows_part = rows_ref[:, pl.ds(pl.multiple_of(z * wide, wide), wide)].astype(F32)
    dots = jnp.sum(x_part * rows_part, axis=1, keepdims=True)
    d_query, d_key, d_value = [], [], []
    for h in range(cols // HEAD_DIM):
        at = slice(h * HEAD_DIM, (h + 1) * HEAD_DIM)
        keys = kvf[:, at]
        values = kvf[:, cols + h * HEAD_DIM : cols + (h + 1) * HEAD_DIM]
        expo = jnp.exp(dot_tt(query[:, at], keys) * scale) * key_mask
        probs = expo / jnp.sum(expo, axis=1, keepdims=True)
        reach = dot_tt(back_b[:, at], values)
        along = jnp.sum(probs * reach, axis=1, keepdims=True)
        dots = dots + along
        d_logits = (probs * (reach - along) * (scale * factor)).astype(BF)
        d_query.append(dot(d_logits, keys))
        d_key.append(dot_00(d_logits, query[:, at]))
        d_value.append(dot_00(probs.astype(BF), scaled_back[:, at]))
    d_query = jnp.concatenate(d_query, axis=1)
    put_blocks(dks, jnp.concatenate(d_key, axis=1), jnp.concatenate(d_value, axis=1))

    eye = lax.broadcasted_iota(jnp.int32, (tgt, tgt), 0) == lax.broadcasted_iota(jnp.int32, (tgt, tgt), 1)
    inner_part = jnp.sum(
        jnp.where(eye, jnp.sum(d_query * q_raw, axis=1, keepdims=True), 0.0), axis=0, keepdims=True
    )
    score_part = jnp.sum(dots * factor, axis=0, keepdims=True)
    line = lax.broadcasted_iota(jnp.int32, (8, 128), 0)
    zt[z] = jnp.where(line == 0, score_part, jnp.where(line == 1, inner_part, 0.0))

    def z_tile(k):
        return remote(zt.at[z], zt.at[z], zss.at[k], zsr.at[k], {"tensor": up(z, k)})

    def c_tile(k):
        return remote(ct.at[c], ct.at[c], css.at[k], csr.at[k], {"cand": up(c, k)})

    def l_tile(k):
        return remote(lt.at[s], lt.at[s], lss.at[k], lsr.at[k], {"source": up(s, k)})

    def dk1(k):
        return cand_all(lambda i: dks.at[i], dkr, d1s, d1r, k)

    def dk2(k):
        return cand_all(lambda i: dko.at[c], dko, d2s, d2r, k)

    def en(k):
        return remote(ens.at[up(z, k)], enr.at[z], ess.at[k], esr.at[k], {"tensor": up(z, k)})

    for k in range(1, N):
        go(z_tile(k))
    for k in range(1, N):
        go(dk1(k))

    dq = d_query.astype(BF)

    def term(dest):
        return dot_tt(dq, wqf[dest])

    def rs_copy(way, hop, chunk):
        part = pl.ds(chunk * step, step)
        return remote(
            rso.at[way, hop - 1, part], rsr.at[way, hop - 1, part],
            rss.at[way, hop - 1, chunk], rsrs.at[way, hop - 1, chunk], {"tensor": up(z, 1 if way == 0 else -1)},
        )

    def rs_round(hop):
        for way in range(2):
            own[way] = term(up(z, hop if way == 0 else -hop))
        fresh = [(w, ch) for w in range(2) for ch in range(CH) if not hop_exists(w, hop + 1, ch)]
        late = [(w, ch) for ch in range(CH) for w in range(2) if hop_exists(w, hop + 1, ch)]
        for way, chunk in fresh + late:
            if not hop_exists(way, hop, chunk):
                continue
            part = pl.ds(chunk * step, step)
            value = own[way, part]
            if hop_exists(way, hop + 1, chunk):
                rs_copy(way, hop + 1, chunk).wait_recv()
                value = value + rsr[way, hop, part].astype(F32)
            rso[way, hop - 1, part] = value.astype(BF)
            go(rs_copy(way, hop, chunk))

    rs_round(4)

    for k in range(1, N):
        z_tile(k).wait_recv()
    sums = zt[0]
    for i in range(1, N):
        sums = sums + zt[i]
    weight = jnp.exp(sums[0:1])
    inner = sums[1:2]
    risk = jnp.full((1, 128), cost_ref[0, 0], jnp.int32).astype(F32) / 100.0
    ct[c] = jnp.where(line == 0, weight, jnp.where(line == 1, risk, 0.0))
    for k in range(1, N):
        go(c_tile(k))

    rs_round(3)

    for k in range(1, N):
        c_tile(k).wait_recv()
    total_w, total_wr = ct[0, 0:1], ct[0, 0:1] * ct[0, 1:2]
    for i in range(1, N):
        total_w = total_w + ct[i, 0:1]
        total_wr = total_wr + ct[i, 0:1] * ct[i, 1:2]
    expected = total_wr / total_w
    lt[s] = jnp.broadcast_to(expected, (8, 128))
    for k in range(1, N):
        go(l_tile(k))
    dkr[c] = dks[c]
    for k in range(1, N):
        dk1(k).wait_recv()
    total = jnp.zeros(dkr.shape[1:], F32)
    for i in range(N):
        share = ct[i, 0:1] / total_w * (ct[i, 1:2] - expected) / N
        total = total + share * dkr[i].astype(F32)
    dko[c] = total.astype(BF)
    for k in range(1, N):
        go(dk2(k))

    rs_round(2)

    for k in range(1, N):
        dk2(k).wait_recv()
    sides = []
    for g in range(4):
        sides.append(jnp.concatenate([dko[g * 2], dko[g * 2 + 1]], axis=0))
    enc_term = dot_tt(jnp.concatenate(sides[:2], axis=1), wk_ref[...])
    enc_term = enc_term + dot_tt(jnp.concatenate(sides[2:], axis=1), wv_ref[...])
    for i in range(N):
        ens[i] = enc_term[i * gpad : (i + 1) * gpad].astype(BF)
    for k in range(1, N):
        go(en(k))

    rs_round(1)

    enr[z] = ens[z]
    for k in range(1, N):
        en(k).wait_recv()
    total = enr[0].astype(F32)
    for i in range(1, N):
        total = total + enr[i].astype(F32)
    genc_ref[...] = total[:group]

    for k in range(1, N):
        l_tile(k).wait_recv()
    loss = lt[0, 0:1]
    for i in range(1, N):
        loss = loss + lt[i, 0:1]
    loss_ref[...] = loss / N

    share = weight / total_w * (risk - expected) / N
    rad_ref[...] = share * inner / jnp.sqrt(jnp.full((1, 128), width, F32))
    share_col = share[:, 0:1]
    inner_col = jnp.sum(jnp.where(eye, inner, 0.0), axis=1, keepdims=True)
    own[0] = term(z)
    for chunk in range(CH):
        for way in range(2):
            rs_copy(way, 1, chunk).wait_recv()
    normed_grad = own[0] + rsr[0, 0].astype(F32) + rsr[1, 0].astype(F32)
    gain_part = gain_ref[:, pl.ds(pl.multiple_of(z * wide, wide), wide)]
    gdec_ref[...] = share_col * (
        factor * rows_part
        + inv_rms * gain_part * normed_grad
        - x_part * (inv_rms * inv_rms * inv_rms * inner_col / width)
    )
    for copy in started:
        copy.wait_send()


def local(
    dec_states, enc_states, norm_gain, w_query, w_key, w_value, w_out, target_rows, cand_lengths, src_lengths, costs
):
    x = dec_states[0, 0]
    enc = enc_states[0]
    tgt, wide = x.shape
    srcs = enc.shape[0]
    depth, cols = w_query.shape
    group = srcs // N
    gpad = -(-group // 16) * 16
    pad = gpad * N
    vmem = pl.BlockSpec(memory_space=pltpu.VMEM)
    smem = pl.BlockSpec(memory_space=pltpu.SMEM)
    dma = pltpu.SemaphoreType.DMA
    block = (N, pad // 2, 128)
    loss, grad_dec, grad_enc, radial = pl.pallas_call(
        kernel,
        out_shape=(
            jax.ShapeDtypeStruct((1, 128), F32),
            jax.ShapeDtypeStruct((tgt, wide), F32),
            jax.ShapeDtypeStruct((group, depth), F32),
            jax.ShapeDtypeStruct((1, tgt), F32),
        ),
        in_specs=[pl.BlockSpec(memory_space=pltpu.HBM)] * 8 + [smem] * 3,
        out_specs=(vmem,) * 4,
        scratch_shapes=[
            pltpu.VMEM(enc.shape, BF),
            pltpu.VMEM((1, wide * N), F32),
            pltpu.VMEM((depth, cols), BF),
            pltpu.VMEM((depth, cols), BF),
            pltpu.VMEM((tgt, wide * N), BF),
            dma((8,)),
            pltpu.VMEM((tgt, wide * N), BF),
            pltpu.VMEM((N, tgt, wide), BF),
            pltpu.VMEM((N, depth, cols), BF),
            pltpu.VMEM((N, cols, depth), BF),
            pltpu.VMEM(block, BF),
            pltpu.VMEM(block, BF),
            pltpu.VMEM(block, BF),
            pltpu.VMEM((pad, 2 * cols), BF),
            pltpu.VMEM(block, BF),
            pltpu.VMEM(block, BF),
            pltpu.VMEM(block, BF),
            pltpu.VMEM((N, 8, 128), F32),
            pltpu.VMEM((N, 8, 128), F32),
            pltpu.VMEM((N, 8, 128), F32),
            pltpu.VMEM((N, gpad, depth), BF),
            pltpu.VMEM((N, gpad, depth), BF),
            pltpu.VMEM((2, 4, tgt, wide), BF),
            pltpu.VMEM((2, 4, tgt, wide), BF),
            pltpu.VMEM((2, tgt, wide), F32),
            dma((2, 4, CH)), dma((2, 4, CH)),
            dma((2, 3)), dma((2, 3)),
            dma((2, 4)), dma((2, 4)),
            dma((2, 7)), dma((2, 7)),
        ]
        + [dma((N,))] * 16
        + [dma((2, 4, CH)), dma((2, 4, CH))],
        compiler_params=pltpu.CompilerParams(
            collective_id=0, has_side_effects=True, vmem_limit_bytes=40 * 1024 * 1024
        ),
    )(
        *(
            pltpu.with_memory_space_constraint(array, pltpu.HBM)
            for array in (x, enc, norm_gain.reshape(1, -1), w_query, w_key, w_value, w_out, target_rows[0, 0])
        ),
        cand_lengths, src_lengths, costs,
    )
    return loss[0, 0], grad_dec[None, None], grad_enc[None], radial[None]


def solution(mesh):
    placed = (
        P("source", "cand", None, "tensor"),
        P("source", None, "cand"),
        P(),
        P("cand", "tensor"),
        P("cand", "tensor"),
        P("cand", "tensor"),
        P("tensor", "cand"),
        P("source", "cand", None, None),
        P("source", "cand"),
        P("source"),
        P("source", "cand"),
    )
    return jax.shard_map(
        local,
        mesh=mesh,
        in_specs=placed,
        out_specs=(
            P(),
            P("source", "cand", None, "tensor"),
            P("source", "tensor", "cand"),
            P("source", "cand", None),
        ),
        check_vma=False,
    )
```

```python
import jax
import jax.numpy as jnp
from jax import lax
from jax.experimental import pallas as pl
from jax.experimental.pallas import tpu as pltpu
from jax.sharding import PartitionSpec as P

HEAD_DIM = 64
N = 8
XS = 4
WCH = 1
CH = 2
MESH = pl.DeviceIdType.MESH
BF = jnp.bfloat16
F32 = jnp.float32


def dot(left, right):
    return jnp.dot(left, right, preferred_element_type=F32)


def dot_tt(left, right):
    return lax.dot_general(left, right, (((1,), (1,)), ((), ())), preferred_element_type=F32)


def dot_00(left, right):
    return lax.dot_general(left, right, (((0,), (0,)), ((), ())), preferred_element_type=F32)


def hop_exists(way, hop, chunk):
    return hop <= 3 or (hop == 4 and (chunk < CH // 2) == (way == 0))


def kernel(
    x_in, enc_in, gain_in, wq_in, wk_in, wv_in, wo_in, rows_in, clen_ref, slen_ref, cost_ref,
    loss_ref, gdec_ref, genc_ref, rad_ref,
    enc_ref, gain_ref, wk_ref, wv_ref, rows_ref, loads, xn, xg, wqf, wof, kvs, kvr, kvo, kvf, dks, dkr, dko, zt, it, ct, lt, ens, enr, rso, rsr, own,
    its, itr, xss, xsr, wxs, wxr, wys, wyr, wss, wsr, k1s, k1r, k2s, k2r, d1s, d1r, d2s, d2r,
    zss, zsr, css, csr, lss, lsr, ess, esr, rss, rsrs,
):
    s, c, z = lax.axis_index("source"), lax.axis_index("cand"), lax.axis_index("tensor")
    core, xx, yl = lax.rem(s, 2), c // 2, lax.rem(c, 2)
    sgn = 1 - 2 * core
    tgt, wide = x_in.shape
    width = wide * N
    cols = wq_in.shape[1]
    srcs = enc_ref.shape[0]
    pad = kvf.shape[0]
    group = srcs // N
    gpad = pad // N

    def up(i, k):
        return lax.rem(i + k + N, N)

    def remote(src, dst, ssem, rsem, dev):
        return pltpu.make_async_remote_copy(
            src_ref=src, dst_ref=dst, send_sem=ssem, recv_sem=rsem, device_id=dev, device_id_type=MESH
        )

    y_to = {"source": up(s, 2 * yl * (1 - core) - 2 * (1 - yl) * core), "cand": c + 1 - 2 * yl}
    y_from = {"source": up(s, 2 * yl * core - 2 * (1 - yl) * (1 - core)), "cand": c + 1 - 2 * yl}

    x_own, wq_own, wo_own = xg.at[z], wqf.at[c], wof.at[c]
    into = (x_own, wq_own, enc_ref, wk_ref, wv_ref, wo_own, rows_ref, gain_ref)
    local_copies = [
        pltpu.make_async_copy(src, dst, loads.at[i])
        for i, (src, dst) in enumerate(zip((x_in, wq_in, enc_in, wk_in, wv_in, wo_in, rows_in, gain_in), into))
    ]
    for copy in local_copies:
        copy.start()
    x_load, wq_load, enc_load, wk_load, wv_load, wo_load, rows_load, gain_load = local_copies

    barrier = pltpu.get_barrier_semaphore()
    for k in range(1, N):
        pl.semaphore_signal(barrier, inc=1, device_id={"tensor": up(z, k)}, device_id_type=MESH)
        pl.semaphore_signal(barrier, inc=1, device_id={"cand": up(c, k)}, device_id_type=MESH)
        pl.semaphore_signal(barrier, inc=1, device_id={"source": up(s, k)}, device_id_type=MESH)
    pl.semaphore_signal(barrier, inc=1, device_id=y_from, device_id_type=MESH)
    pl.semaphore_wait(barrier, 3 * (N - 1) + 1)

    started = []
    far_z, far_c = (4, 3, 5, 2, 6, 1, 7), (5, 4, 3, 2, 6, 7, 1)

    def go(copy):
        copy.start()
        started.append(copy)

    def drain(keep=0):
        done = started[: len(started) - keep]
        del started[: len(started) - keep]
        for copy in done:
            copy.wait_send()

    step = tgt // CH

    def x_copy(way, hop, chunk):
        to = 1 if way == 0 else -1
        block = up(z, -to * (hop - 1))
        part = pl.ds(chunk * step, step)
        src = x_in.at[part] if hop == 1 else xg.at[block, part]
        return remote(src, xg.at[block, part], xss.at[way, hop - 1, chunk], xsr.at[way, hop - 1, chunk], {"tensor": up(z, to)})

    def x_round(hop):
        for chunk in range(CH):
            for way in range(2):
                if hop_exists(way, hop, chunk):
                    x_copy(way, hop, chunk).wait_recv()
                    if hop_exists(way, hop + 1, chunk):
                        go(x_copy(way, hop + 1, chunk))

    hq, ho = wq_in.shape[0] // (2 * WCH), wo_in.shape[0] // (2 * WCH)
    mine = [wq_in] * WCH + [wo_in] * WCH
    full, half = [], []
    for j in range(WCH):
        half.append(pl.ds(pl.multiple_of((core * WCH + j) * hq, hq), hq))
        full.append(wqf)
    for j in range(WCH):
        half.append(pl.ds(pl.multiple_of((core * WCH + j) * ho, ho), ho))
        full.append(wof)

    def piece(dx, dy):
        return lax.rem(xx + dx + XS, XS) * 2 + (yl if dy == 0 else 1 - yl)

    def x_dev(to):
        return {"cand": lax.rem(xx + to + XS, XS) * 2 + yl}

    def w_own(m, i):
        return remote(mine[m].at[half[m]], full[m].at[c, half[m]], wxs.at[m, i], wxr.at[m, i], x_dev(1 - 2 * i))

    def w_relay(m):
        there = full[m].at[piece(-sgn, 0), half[m]]
        return remote(there, there, wxs.at[m, 2], wxr.at[m, 2], x_dev(sgn))

    def w_x_wait(m, i):
        there = full[m].at[c, half[m]]
        remote(there, there, wxs.at[m, i], wxr.at[m, i], x_dev(1)).wait_recv()

    hops = (0, -sgn, sgn, 2)

    def w_y(m, i):
        there = full[m].at[piece(hops[i], 0), half[m]]
        return remote(mine[m].at[half[m]] if i == 0 else there, there, wys.at[m, i], wyr.at[m, i], y_to)

    def w_sib(m, i):
        there = full[m].at[piece(hops[i % 4], i // 4), half[m]]
        return remote(there, there, wss.at[m, i - 1], wsr.at[m, i - 1], {"source": s + sgn})

    def w_near(m):
        w_x_wait(m, core)
        go(w_relay(m))
        go(w_y(m, 1))
        go(w_sib(m, 1))
        w_x_wait(m, 1 - core)
        go(w_y(m, 2))
        go(w_sib(m, 2))

    def w_across(m):
        w_y(m, 0).wait_recv()
        go(w_sib(m, 4))

    def w_far(m):
        w_relay(m).wait_recv()
        go(w_y(m, 3))
        go(w_sib(m, 3))

    def w_corner(m):
        for i in (1, 2):
            w_y(m, i).wait_recv()
            go(w_sib(m, 4 + i))

    def w_end(m):
        w_y(m, 3).wait_recv()
        go(w_sib(m, 7))

    def w_got(m, i):
        w_sib(m, i).wait_recv()

    firsts, seconds = range(WCH), range(WCH, 2 * WCH)

    def w_start(m):
        for i in range(2):
            go(w_own(m, i))
        go(w_y(m, 0))

    for chunk in range(CH):
        for way in range(2):
            go(x_copy(way, 1, chunk))
    for m in range(2 * WCH):
        w_start(m)

    row = lax.broadcasted_iota(jnp.int32, (pad, srcs), 0)
    col = lax.broadcasted_iota(jnp.int32, (pad, srcs), 1)
    spot = lax.rem(row, gpad)
    spread = jnp.where((spot < group) & (row // gpad * group + spot == col), 1.0, 0.0).astype(BF)
    enc_load.wait()
    wk_load.wait()
    wv_load.wait()
    enc = dot(spread, enc_ref[...]).astype(BF)
    k_part = dot(enc, wk_ref[...])
    v_part = dot(enc, wv_ref[...])

    def put_blocks(dst, left, right):
        for g in range(4):
            src = (left if g < 2 else right)[:, (g % 2) * 128 : (g % 2) * 128 + 128].astype(BF)
            for r in range(2):
                dst[g * 2 + r] = src[r * (pad // 2) : (r + 1) * (pad // 2)]

    def cand_all(send_of, dst, ssem, rsem, k):
        return remote(send_of(up(c, k)), dst.at[c], ssem.at[k], rsem.at[k], {"cand": up(c, k)})

    put_blocks(kvs, k_part, v_part)

    def kv1(k):
        return cand_all(lambda i: kvs.at[i], kvr, k1s, k1r, k)

    def kv2(k):
        return cand_all(lambda i: kvo.at[c], kvo, k2s, k2r, k)

    for k in far_c:
        go(kv1(k))
    gain_load.wait()
    rows_load.wait()

    def gained(b):
        block = xg[b].astype(F32)
        xn[:, pl.ds(pl.multiple_of(b * wide, wide), wide)] = (
            block * gain_ref[:, pl.ds(pl.multiple_of(b * wide, wide), wide)]
        ).astype(BF)
        return jnp.sum(block * block, axis=1, keepdims=True)

    def r_term(b):
        return dot_tt(rows_ref[:, pl.ds(pl.multiple_of(b * wide, wide), wide)], wof[b])

    wq_load.wait()
    wo_load.wait()
    x_load.wait()
    squares = gained(z)
    w_across(0)
    x_round(1)
    w_near(0)
    w_across(1)
    x_round(2)
    w_near(1)
    kvr[c] = kvs[c]
    for k in range(1, N):
        kv1(k).wait_recv()
    total = kvr[0].astype(F32)
    for i in range(1, N):
        total = total + kvr[i].astype(F32)
    kvo[c] = total.astype(BF)
    for k in far_c:
        go(kv2(k))
    w_far(0)
    x_round(3)
    w_corner(0)
    w_far(1)
    squares = squares + gained(up(z, 1)) + gained(up(z, -1)) + gained(up(z, 2)) + gained(up(z, -2))
    back = r_term(c)
    w_corner(1)
    for i in (1, 2, 4):
        w_got(1, i)
    back = back + r_term(piece(0, 1)) + r_term(piece(1, 0)) + r_term(piece(-1, 0))
    x_round(4)
    squares = squares + gained(up(z, 3)) + gained(up(z, -3))
    w_end(0)
    w_got(1, 3)
    back = back + r_term(piece(2, 0))
    w_got(1, 5)
    w_got(1, 6)
    back = back + r_term(piece(1, 1)) + r_term(piece(-1, 1))
    w_end(1)
    squares = squares + gained(up(z, 4))
    for k in range(1, N):
        kv2(k).wait_recv()
    for g in range(4):
        for r in range(2):
            kvf[r * (pad // 2) : (r + 1) * (pad // 2), g * 128 : (g + 1) * 128] = kvo[g * 2 + r]
    for i in range(1, N):
        w_got(0, i)
    q_raw = jnp.zeros((tgt, cols), F32)
    for b in range(N):
        q_raw = q_raw + dot(xn[:, b * wide : (b + 1) * wide], wqf[b])
    inv_rms = lax.rsqrt(squares / width + 1e-06)
    query = (q_raw * inv_rms).astype(BF)
    w_got(1, 7)
    back = back + r_term(piece(2, 1))
    back_b = back.astype(BF)

    length = jnp.full((tgt, 1), clen_ref[0, 0], jnp.int32)
    inside = (lax.broadcasted_iota(jnp.int32, (tgt, 1), 0) < length).astype(F32)
    factor = inside / jnp.sqrt(width * length.astype(F32))
    place = lax.broadcasted_iota(jnp.int32, (1, pad), 1)
    spot = lax.rem(place, gpad)
    real = (spot < group) & (place // gpad * group + spot < jnp.full((1, pad), slen_ref[0], jnp.int32))
    key_mask = real.astype(F32)
    scale = HEAD_DIM ** (-0.5)
    x_part = xg[z].astype(F32)
    rows_part = rows_ref[:, pl.ds(pl.multiple_of(z * wide, wide), wide)].astype(F32)
    dots = jnp.sum(x_part * rows_part, axis=1, keepdims=True)
    eye = lax.broadcasted_iota(jnp.int32, (tgt, tgt), 0) == lax.broadcasted_iota(jnp.int32, (tgt, tgt), 1)
    line = lax.broadcasted_iota(jnp.int32, (8, 128), 0)

    heads = [slice(h * HEAD_DIM, (h + 1) * HEAD_DIM) for h in range(cols // HEAD_DIM)]
    probs = []
    for at in heads:
        expo = jnp.exp(dot_tt(query[:, at], kvf[:, at]) * scale) * key_mask
        probs.append(expo / jnp.sum(expo, axis=1, keepdims=True))
    reach, along = [], []
    for h, at in enumerate(heads):
        reach.append(dot_tt(back_b[:, at], kvf[:, cols + h * HEAD_DIM : cols + (h + 1) * HEAD_DIM]))
        along.append(jnp.sum(probs[h] * reach[h], axis=1, keepdims=True))
        dots = dots + along[h]
    score_part = jnp.sum(dots * factor, axis=0, keepdims=True)
    zt[z] = jnp.broadcast_to(score_part, (8, 128))

    def z_tile(k):
        return remote(zt.at[z], zt.at[z], zss.at[k], zsr.at[k], {"tensor": up(z, k)})

    def c_tile(k):
        return remote(ct.at[c], ct.at[c], css.at[k], csr.at[k], {"cand": up(c, k)})

    def l_tile(k):
        return remote(lt.at[s], lt.at[s], lss.at[k], lsr.at[k], {"source": up(s, k)})

    def dk1(k):
        return cand_all(lambda i: dks.at[i], dkr, d1s, d1r, k)

    def dk2(k):
        return cand_all(lambda i: dko.at[c], dko, d2s, d2r, k)

    def en(k):
        return remote(ens.at[up(z, k)], enr.at[z], ess.at[k], esr.at[k], {"tensor": up(z, k)})

    def i_tile(k):
        return remote(it.at[z], it.at[z], its.at[k], itr.at[k], {"tensor": up(z, k)})

    for k in far_z:
        go(z_tile(k))

    d_logits, d_query = [], []
    for h, at in enumerate(heads):
        d_logits.append((probs[h] * (reach[h] - along[h]) * (scale * factor)).astype(BF))
        d_query.append(dot(d_logits[h], kvf[:, at]))
    d_query = jnp.concatenate(d_query, axis=1)

    dq = d_query.astype(BF)

    def term(dest):
        return dot_tt(dq, wqf[dest])

    def rs_copy(way, hop, chunk):
        part = pl.ds(chunk * step, step)
        return remote(
            rso.at[way, hop - 1, part], rsr.at[way, hop - 1, part],
            rss.at[way, hop - 1, chunk], rsrs.at[way, hop - 1, chunk], {"tensor": up(z, 1 if way == 0 else -1)},
        )

    def rs_round(hop):
        own[0] = term(up(z, hop))
        if hop < 4:
            own[1] = term(up(z, -hop))
        fresh = [(w, ch) for w in range(2) for ch in range(CH) if not hop_exists(w, hop + 1, ch)]
        late = [(w, ch) for ch in range(CH) for w in range(2) if hop_exists(w, hop + 1, ch)]
        for way, chunk in fresh + late:
            if not hop_exists(way, hop, chunk):
                continue
            part = pl.ds(chunk * step, step)
            value = own[way if hop < 4 else 0, part]
            if hop_exists(way, hop + 1, chunk):
                rs_copy(way, hop + 1, chunk).wait_recv()
                value = value + rsr[way, hop, part].astype(F32)
            rso[way, hop - 1, part] = value.astype(BF)
            go(rs_copy(way, hop, chunk))

    rs_round(4)

    scaled_back = (back * factor).astype(BF)
    d_key, d_value = [], []
    for h, at in enumerate(heads):
        d_key.append(dot_00(d_logits[h], query[:, at]))
        d_value.append(dot_00(probs[h].astype(BF), scaled_back[:, at]))
    put_blocks(dks, jnp.concatenate(d_key, axis=1), jnp.concatenate(d_value, axis=1))
    for k in far_c:
        go(dk1(k))
    inner_part = jnp.sum(
        jnp.where(eye, jnp.sum(d_query * q_raw, axis=1, keepdims=True), 0.0), axis=0, keepdims=True
    )
    it[z] = jnp.broadcast_to(inner_part, (8, 128))
    for k in far_z:
        go(i_tile(k))

    for k in range(1, N):
        z_tile(k).wait_recv()
    score = zt[0, 0:1]
    for i in range(1, N):
        score = score + zt[i, 0:1]
    weight = jnp.exp(score)
    risk = jnp.full((1, 128), cost_ref[0, 0], jnp.int32).astype(F32) / 100.0
    ct[c] = jnp.where(line == 0, weight, jnp.where(line == 1, risk, 0.0))
    for k in far_c:
        go(c_tile(k))
    drain(4 * N)

    rs_round(3)

    for k in range(1, N):
        c_tile(k).wait_recv()
    total_w, total_wr = ct[0, 0:1], ct[0, 0:1] * ct[0, 1:2]
    for i in range(1, N):
        total_w = total_w + ct[i, 0:1]
        total_wr = total_wr + ct[i, 0:1] * ct[i, 1:2]
    expected = total_wr / total_w
    dkr[c] = dks[c]
    for k in range(1, N):
        dk1(k).wait_recv()
    total = jnp.zeros(dkr.shape[1:], F32)
    for i in range(N):
        share = ct[i, 0:1] / total_w * (ct[i, 1:2] - expected) / N
        total = total + share * dkr[i].astype(F32)
    dko[c] = total.astype(BF)
    for k in far_c:
        go(dk2(k))
    lt[s] = jnp.broadcast_to(expected, (8, 128))
    for k in range(1, N):
        go(l_tile(k))

    drain(2 * N)
    rs_round(2)

    for k in range(1, N):
        dk2(k).wait_recv()
    sides = []
    for g in range(4):
        sides.append(jnp.concatenate([dko[g * 2], dko[g * 2 + 1]], axis=0))
    enc_term = dot_tt(jnp.concatenate(sides[:2], axis=1), wk_ref[...])
    enc_term = enc_term + dot_tt(jnp.concatenate(sides[2:], axis=1), wv_ref[...])
    for i in range(N):
        ens[i] = enc_term[i * gpad : (i + 1) * gpad].astype(BF)
    for k in far_z:
        go(en(k))
    enr[z] = ens[z]
    drain(2 * N)

    rs_round(1)

    for k in range(1, N):
        i_tile(k).wait_recv()
    inner = it[0, 0:1]
    for i in range(1, N):
        inner = inner + it[i, 0:1]
    share = weight / total_w * (risk - expected) / N
    rad_ref[...] = share * inner / jnp.sqrt(jnp.full((1, 128), width, F32))
    share_col = share[:, 0:1]
    inner_col = jnp.sum(jnp.where(eye, inner, 0.0), axis=1, keepdims=True)
    own[0] = term(z)
    for chunk in range(CH):
        for way in range(2):
            rs_copy(way, 1, chunk).wait_recv()
    normed_grad = own[0] + rsr[0, 0].astype(F32) + rsr[1, 0].astype(F32)
    gain_part = gain_ref[:, pl.ds(pl.multiple_of(z * wide, wide), wide)]
    gdec_ref[...] = share_col * (
        factor * rows_part
        + inv_rms * gain_part * normed_grad
        - x_part * (inv_rms * inv_rms * inv_rms * inner_col / width)
    )
    for k in range(1, N):
        l_tile(k).wait_recv()
    loss = lt[0, 0:1]
    for i in range(1, N):
        loss = loss + lt[i, 0:1]
    loss_ref[...] = loss / N
    for k in range(1, N):
        en(k).wait_recv()
    total = enr[0].astype(F32)
    for i in range(1, N):
        total = total + enr[i].astype(F32)
    genc_ref[...] = total[:group]
    drain()


def local(
    dec_states, enc_states, norm_gain, w_query, w_key, w_value, w_out, target_rows, cand_lengths, src_lengths, costs
):
    x = dec_states[0, 0]
    enc = enc_states[0]
    tgt, wide = x.shape
    srcs = enc.shape[0]
    depth, cols = w_query.shape
    group = srcs // N
    gpad = -(-group // 16) * 16
    pad = gpad * N
    vmem = pl.BlockSpec(memory_space=pltpu.VMEM)
    smem = pl.BlockSpec(memory_space=pltpu.SMEM)
    dma = pltpu.SemaphoreType.DMA
    block = (N, pad // 2, 128)
    loss, grad_dec, grad_enc, radial = pl.pallas_call(
        kernel,
        out_shape=(
            jax.ShapeDtypeStruct((1, 128), F32),
            jax.ShapeDtypeStruct((tgt, wide), F32),
            jax.ShapeDtypeStruct((group, depth), F32),
            jax.ShapeDtypeStruct((1, tgt), F32),
        ),
        in_specs=[pl.BlockSpec(memory_space=pltpu.HBM)] * 8 + [smem] * 3,
        out_specs=(vmem,) * 4,
        scratch_shapes=[
            pltpu.VMEM(enc.shape, BF),
            pltpu.VMEM((1, wide * N), F32),
            pltpu.VMEM((depth, cols), BF),
            pltpu.VMEM((depth, cols), BF),
            pltpu.VMEM((tgt, wide * N), BF),
            dma((8,)),
            pltpu.VMEM((tgt, wide * N), BF),
            pltpu.VMEM((N, tgt, wide), BF),
            pltpu.VMEM((N, depth, cols), BF),
            pltpu.VMEM((N, cols, depth), BF),
            pltpu.VMEM(block, BF),
            pltpu.VMEM(block, BF),
            pltpu.VMEM(block, BF),
            pltpu.VMEM((pad, 2 * cols), BF),
            pltpu.VMEM(block, BF),
            pltpu.VMEM(block, BF),
            pltpu.VMEM(block, BF),
            pltpu.VMEM((N, 8, 128), F32),
            pltpu.VMEM((N, 8, 128), F32),
            pltpu.VMEM((N, 8, 128), F32),
            pltpu.VMEM((N, 8, 128), F32),
            pltpu.VMEM((N, gpad, depth), BF),
            pltpu.VMEM((N, gpad, depth), BF),
            pltpu.VMEM((2, 4, tgt, wide), BF),
            pltpu.VMEM((2, 4, tgt, wide), BF),
            pltpu.VMEM((2, tgt, wide), F32),
            dma((N,)), dma((N,)),
            dma((2, 4, CH)), dma((2, 4, CH)),
            dma((2 * WCH, 4)), dma((2 * WCH, 4)),
            dma((2 * WCH, 4)), dma((2 * WCH, 4)),
            dma((2 * WCH, 7)), dma((2 * WCH, 7)),
        ]
        + [dma((N,))] * 16
        + [dma((2, 4, CH)), dma((2, 4, CH))],
        compiler_params=pltpu.CompilerParams(
            collective_id=0, has_side_effects=True, vmem_limit_bytes=40 * 1024 * 1024
        ),
    )(
        *(
            pltpu.with_memory_space_constraint(array, pltpu.HBM)
            for array in (x, enc, norm_gain.reshape(1, -1), w_query, w_key, w_value, w_out, target_rows[0, 0])
        ),
        cand_lengths, src_lengths, costs,
    )
    return loss[0, 0], grad_dec[None, None], grad_enc[None], radial[None]


def solution(mesh):
    placed = (
        P("source", "cand", None, "tensor"),
        P("source", None, "cand"),
        P(),
        P("cand", "tensor"),
        P("cand", "tensor"),
        P("cand", "tensor"),
        P("tensor", "cand"),
        P("source", "cand", None, None),
        P("source", "cand"),
        P("source"),
        P("source", "cand"),
    )
    return jax.shard_map(
        local,
        mesh=mesh,
        in_specs=placed,
        out_specs=(
            P(),
            P("source", "cand", None, "tensor"),
            P("source", "tensor", "cand"),
            P("source", "cand", None),
        ),
        check_vma=False,
    )
```

```python
import jax
import jax.numpy as jnp
from jax import lax
from jax.experimental import pallas as pl
from jax.experimental.pallas import tpu as pltpu
from jax.sharding import PartitionSpec as P

HEAD_DIM = 64
N = 8
XS = 4
WCH = 1
CH = 2
MESH = pl.DeviceIdType.MESH
BF = jnp.bfloat16
F32 = jnp.float32


def dot(left, right):
    return jnp.dot(left, right, preferred_element_type=F32)


def dot_tt(left, right):
    return lax.dot_general(left, right, (((1,), (1,)), ((), ())), preferred_element_type=F32)


def dot_00(left, right):
    return lax.dot_general(left, right, (((0,), (0,)), ((), ())), preferred_element_type=F32)


def hop_exists(way, hop, chunk):
    return hop <= 3 or (hop == 4 and (chunk < CH // 2) == (way == 0))


def kernel(
    x_in, enc_in, gain_in, wq_in, wk_in, wv_in, wo_in, rows_in, clen_ref, slen_ref, cost_ref,
    loss_ref, gdec_ref, genc_ref, rad_ref,
    enc_ref, gain_ref, wk_ref, wv_ref, rows_ref, loads, xn, xg, wqf, wof, kvs, kvr, kvo, kvf, dks, dkr, dko, zt, it, ct, lt, ens, enr, rso, rsr, own,
    its, itr, xss, xsr, wxs, wxr, wys, wyr, wss, wsr, k1s, k1r, k2s, k2r, d1s, d1r, d2s, d2r,
    zss, zsr, css, csr, lss, lsr, ess, esr, rss, rsrs,
):
    s, c, z = lax.axis_index("source"), lax.axis_index("cand"), lax.axis_index("tensor")
    core, xx, yl = lax.rem(s, 2), c // 2, lax.rem(c, 2)
    sgn = 1 - 2 * core
    tgt, wide = x_in.shape
    width = wide * N
    cols = wq_in.shape[1]
    srcs = enc_ref.shape[0]
    pad = kvf.shape[0]
    group = srcs // N
    gpad = pad // N

    def up(i, k):
        return lax.rem(i + k + N, N)

    def remote(src, dst, ssem, rsem, dev):
        return pltpu.make_async_remote_copy(
            src_ref=src, dst_ref=dst, send_sem=ssem, recv_sem=rsem, device_id=dev, device_id_type=MESH
        )

    y_to = {"source": up(s, 2 * yl * (1 - core) - 2 * (1 - yl) * core), "cand": c + 1 - 2 * yl}
    y_from = {"source": up(s, 2 * yl * core - 2 * (1 - yl) * (1 - core)), "cand": c + 1 - 2 * yl}

    barrier = pltpu.get_barrier_semaphore()
    for k in range(1, N):
        pl.semaphore_signal(barrier, inc=1, device_id={"tensor": up(z, k)}, device_id_type=MESH)
        pl.semaphore_signal(barrier, inc=1, device_id={"cand": up(c, k)}, device_id_type=MESH)
        pl.semaphore_signal(barrier, inc=1, device_id={"source": up(s, k)}, device_id_type=MESH)
    pl.semaphore_signal(barrier, inc=1, device_id=y_from, device_id_type=MESH)
    x_own, wq_own, wo_own = xg.at[z], wqf.at[c], wof.at[c]
    into = (x_own, wq_own, enc_ref, wk_ref, wv_ref, wo_own, rows_ref, gain_ref)
    local_copies = [
        pltpu.make_async_copy(src, dst, loads.at[i])
        for i, (src, dst) in enumerate(zip((x_in, wq_in, enc_in, wk_in, wv_in, wo_in, rows_in, gain_in), into))
    ]
    for copy in local_copies:
        copy.start()
    x_load, wq_load, enc_load, wk_load, wv_load, wo_load, rows_load, gain_load = local_copies
    pl.semaphore_wait(barrier, 3 * (N - 1) + 1)

    started = []
    far_z, far_c = (4, 3, 5, 2, 6, 1, 7), (5, 4, 3, 2, 6, 7, 1)

    def go(copy):
        copy.start()
        started.append(copy)

    def drain(keep=0):
        done = started[: len(started) - keep]
        del started[: len(started) - keep]
        for copy in done:
            copy.wait_send()

    step = tgt // CH

    def x_copy(way, hop, chunk):
        to = 1 if way == 0 else -1
        block = up(z, -to * (hop - 1))
        part = pl.ds(chunk * step, step)
        src = x_in.at[part] if hop == 1 else xg.at[block, part]
        return remote(src, xg.at[block, part], xss.at[way, hop - 1, chunk], xsr.at[way, hop - 1, chunk], {"tensor": up(z, to)})

    def x_round(hop):
        for chunk in range(CH):
            for way in range(2):
                if hop_exists(way, hop, chunk):
                    x_copy(way, hop, chunk).wait_recv()
                    if hop_exists(way, hop + 1, chunk):
                        go(x_copy(way, hop + 1, chunk))

    hq, ho = wq_in.shape[0] // (2 * WCH), wo_in.shape[0] // (2 * WCH)
    mine = [wq_in] * WCH + [wo_in] * WCH
    full, half = [], []
    for j in range(WCH):
        half.append(pl.ds(pl.multiple_of((core * WCH + j) * hq, hq), hq))
        full.append(wqf)
    for j in range(WCH):
        half.append(pl.ds(pl.multiple_of((core * WCH + j) * ho, ho), ho))
        full.append(wof)

    def piece(dx, dy):
        return lax.rem(xx + dx + XS, XS) * 2 + (yl if dy == 0 else 1 - yl)

    def x_dev(to):
        return {"cand": lax.rem(xx + to + XS, XS) * 2 + yl}

    def w_own(m, i):
        return remote(mine[m].at[half[m]], full[m].at[c, half[m]], wxs.at[m, i], wxr.at[m, i], x_dev(1 - 2 * i))

    def w_relay(m):
        there = full[m].at[piece(-sgn, 0), half[m]]
        return remote(there, there, wxs.at[m, 2], wxr.at[m, 2], x_dev(sgn))

    def w_x_wait(m, i):
        there = full[m].at[c, half[m]]
        remote(there, there, wxs.at[m, i], wxr.at[m, i], x_dev(1)).wait_recv()

    hops = (0, -sgn, sgn, 2)

    def w_y(m, i):
        there = full[m].at[piece(hops[i], 0), half[m]]
        return remote(mine[m].at[half[m]] if i == 0 else there, there, wys.at[m, i], wyr.at[m, i], y_to)

    def w_sib(m, i):
        there = full[m].at[piece(hops[i % 4], i // 4), half[m]]
        return remote(there, there, wss.at[m, i - 1], wsr.at[m, i - 1], {"source": s + sgn})

    def w_near(m):
        w_x_wait(m, core)
        go(w_relay(m))
        go(w_y(m, 1))
        go(w_sib(m, 1))
        w_x_wait(m, 1 - core)
        go(w_y(m, 2))
        go(w_sib(m, 2))

    def w_across(m):
        w_y(m, 0).wait_recv()
        go(w_sib(m, 4))

    def w_far(m):
        w_relay(m).wait_recv()
        go(w_y(m, 3))
        go(w_sib(m, 3))

    def w_corner(m):
        for i in (1, 2):
            w_y(m, i).wait_recv()
            go(w_sib(m, 4 + i))

    def w_end(m):
        w_y(m, 3).wait_recv()
        go(w_sib(m, 7))

    def w_got(m, i):
        w_sib(m, i).wait_recv()

    firsts, seconds = range(WCH), range(WCH, 2 * WCH)

    def w_start(m):
        for i in range(2):
            go(w_own(m, i))
        go(w_y(m, 0))

    for chunk in range(CH):
        for way in range(2):
            go(x_copy(way, 1, chunk))
    for m in range(2 * WCH):
        w_start(m)

    row = lax.broadcasted_iota(jnp.int32, (pad, srcs), 0)
    col = lax.broadcasted_iota(jnp.int32, (pad, srcs), 1)
    spot = lax.rem(row, gpad)
    spread = jnp.where((spot < group) & (row // gpad * group + spot == col), 1.0, 0.0).astype(BF)
    enc_load.wait()
    wk_load.wait()
    wv_load.wait()
    enc = dot(spread, enc_ref[...]).astype(BF)
    k_part = dot(enc, wk_ref[...])
    v_part = dot(enc, wv_ref[...])

    def put_blocks(dst, left, right):
        for g in range(4):
            src = (left if g < 2 else right)[:, (g % 2) * 128 : (g % 2) * 128 + 128].astype(BF)
            for r in range(2):
                dst[g * 2 + r] = src[r * (pad // 2) : (r + 1) * (pad // 2)]

    def cand_all(send_of, dst, ssem, rsem, k):
        return remote(send_of(up(c, k)), dst.at[c], ssem.at[k], rsem.at[k], {"cand": up(c, k)})

    put_blocks(kvs, k_part, v_part)

    def kv1(k):
        return cand_all(lambda i: kvs.at[i], kvr, k1s, k1r, k)

    def kv2(k):
        return cand_all(lambda i: kvo.at[c], kvo, k2s, k2r, k)

    for k in far_c:
        go(kv1(k))
    gain_load.wait()
    rows_load.wait()

    def gained(b):
        block = xg[b].astype(F32)
        xn[:, pl.ds(pl.multiple_of(b * wide, wide), wide)] = (
            block * gain_ref[:, pl.ds(pl.multiple_of(b * wide, wide), wide)]
        ).astype(BF)
        return jnp.sum(block * block, axis=1, keepdims=True)

    def r_term(b):
        return dot_tt(rows_ref[:, pl.ds(pl.multiple_of(b * wide, wide), wide)], wof[b])

    def q_term(b):
        return dot(xn[:, pl.ds(pl.multiple_of(b * wide, wide), wide)], wqf[b])

    wq_load.wait()
    wo_load.wait()
    x_load.wait()
    squares = gained(z)
    w_across(0)
    x_round(1)
    w_near(0)
    w_across(1)
    x_round(2)
    w_near(1)
    kvr[c] = kvs[c]
    for k in range(1, N):
        kv1(k).wait_recv()
    total = kvr[0].astype(F32)
    for i in range(1, N):
        total = total + kvr[i].astype(F32)
    kvo[c] = total.astype(BF)
    for k in far_c:
        go(kv2(k))
    w_far(0)
    x_round(3)
    w_corner(0)
    w_far(1)
    squares = squares + gained(up(z, 1)) + gained(up(z, -1)) + gained(up(z, 2)) + gained(up(z, -2))
    back = r_term(c)
    w_corner(1)
    for i in (1, 2, 4):
        w_got(1, i)
    back = back + r_term(piece(0, 1)) + r_term(piece(1, 0)) + r_term(piece(-1, 0))
    x_round(4)
    squares = squares + gained(up(z, 3)) + gained(up(z, -3)) + gained(up(z, 4))
    for i in (1, 2, 4):
        w_got(0, i)
    q_raw = q_term(c) + q_term(piece(0, 1)) + q_term(piece(1, 0)) + q_term(piece(-1, 0))
    w_end(0)
    w_end(1)
    w_got(1, 3)
    w_got(1, 5)
    w_got(1, 6)
    back = back + r_term(piece(2, 0)) + r_term(piece(1, 1)) + r_term(piece(-1, 1))
    w_got(0, 3)
    w_got(0, 5)
    w_got(0, 6)
    q_raw = q_raw + q_term(piece(2, 0)) + q_term(piece(1, 1)) + q_term(piece(-1, 1))
    for k in range(1, N):
        kv2(k).wait_recv()
    for g in range(4):
        for r in range(2):
            kvf[r * (pad // 2) : (r + 1) * (pad // 2), g * 128 : (g + 1) * 128] = kvo[g * 2 + r]
    w_got(0, 7)
    q_raw = q_raw + q_term(piece(2, 1))
    inv_rms = lax.rsqrt(squares / width + 1e-06)
    query = (q_raw * inv_rms).astype(BF)
    w_got(1, 7)
    back = back + r_term(piece(2, 1))
    back_b = back.astype(BF)

    length = jnp.full((tgt, 1), clen_ref[0, 0], jnp.int32)
    inside = (lax.broadcasted_iota(jnp.int32, (tgt, 1), 0) < length).astype(F32)
    factor = inside / jnp.sqrt(width * length.astype(F32))
    place = lax.broadcasted_iota(jnp.int32, (1, pad), 1)
    spot = lax.rem(place, gpad)
    real = (spot < group) & (place // gpad * group + spot < jnp.full((1, pad), slen_ref[0], jnp.int32))
    key_mask = real.astype(F32)
    scale = HEAD_DIM ** (-0.5)
    x_part = xg[z].astype(F32)
    rows_part = rows_ref[:, pl.ds(pl.multiple_of(z * wide, wide), wide)].astype(F32)
    dots = jnp.sum(x_part * rows_part, axis=1, keepdims=True)
    eye = lax.broadcasted_iota(jnp.int32, (tgt, tgt), 0) == lax.broadcasted_iota(jnp.int32, (tgt, tgt), 1)
    line = lax.broadcasted_iota(jnp.int32, (8, 128), 0)

    heads = [slice(h * HEAD_DIM, (h + 1) * HEAD_DIM) for h in range(cols // HEAD_DIM)]
    probs = []
    for at in heads:
        expo = jnp.exp(dot_tt(query[:, at], kvf[:, at]) * scale) * key_mask
        probs.append(expo / jnp.sum(expo, axis=1, keepdims=True))
    reach, along = [], []
    for h, at in enumerate(heads):
        reach.append(dot_tt(back_b[:, at], kvf[:, cols + h * HEAD_DIM : cols + (h + 1) * HEAD_DIM]))
        along.append(jnp.sum(probs[h] * reach[h], axis=1, keepdims=True))
        dots = dots + along[h]
    score_part = jnp.sum(dots * factor, axis=0, keepdims=True)
    zt[z] = jnp.broadcast_to(score_part, (8, 128))

    def z_tile(k):
        return remote(zt.at[z], zt.at[z], zss.at[k], zsr.at[k], {"tensor": up(z, k)})

    def c_tile(k):
        return remote(ct.at[c], ct.at[c], css.at[k], csr.at[k], {"cand": up(c, k)})

    def l_tile(k):
        return remote(lt.at[s], lt.at[s], lss.at[k], lsr.at[k], {"source": up(s, k)})

    def dk1(k):
        return cand_all(lambda i: dks.at[i], dkr, d1s, d1r, k)

    def dk2(k):
        return cand_all(lambda i: dko.at[c], dko, d2s, d2r, k)

    def en(k):
        return remote(ens.at[up(z, k)], enr.at[z], ess.at[k], esr.at[k], {"tensor": up(z, k)})

    def i_tile(k):
        return remote(it.at[z], it.at[z], its.at[k], itr.at[k], {"tensor": up(z, k)})

    for k in far_z:
        go(z_tile(k))

    d_logits, d_query = [], []
    for h, at in enumerate(heads):
        d_logits.append((probs[h] * (reach[h] - along[h]) * (scale * factor)).astype(BF))
        d_query.append(dot(d_logits[h], kvf[:, at]))
    d_query = jnp.concatenate(d_query, axis=1)

    dq = d_query.astype(BF)

    def term(dest):
        return dot_tt(dq, wqf[dest])

    def rs_copy(way, hop, chunk):
        part = pl.ds(chunk * step, step)
        return remote(
            rso.at[way, hop - 1, part], rsr.at[way, hop - 1, part],
            rss.at[way, hop - 1, chunk], rsrs.at[way, hop - 1, chunk], {"tensor": up(z, 1 if way == 0 else -1)},
        )

    def rs_round(hop):
        own[0] = term(up(z, hop))
        if hop < 4:
            own[1] = term(up(z, -hop))
        fresh = [(w, ch) for w in range(2) for ch in range(CH) if not hop_exists(w, hop + 1, ch)]
        late = [(w, ch) for ch in range(CH) for w in range(2) if hop_exists(w, hop + 1, ch)]
        for way, chunk in fresh + late:
            if not hop_exists(way, hop, chunk):
                continue
            part = pl.ds(chunk * step, step)
            value = own[way if hop < 4 else 0, part]
            if hop_exists(way, hop + 1, chunk):
                rs_copy(way, hop + 1, chunk).wait_recv()
                value = value + rsr[way, hop, part].astype(F32)
            rso[way, hop - 1, part] = value.astype(BF)
            go(rs_copy(way, hop, chunk))

    rs_round(4)

    scaled_back = (back * factor).astype(BF)
    d_key, d_value = [], []
    for h, at in enumerate(heads):
        d_key.append(dot_00(d_logits[h], query[:, at]))
        d_value.append(dot_00(probs[h].astype(BF), scaled_back[:, at]))
    put_blocks(dks, jnp.concatenate(d_key, axis=1), jnp.concatenate(d_value, axis=1))
    for k in far_c:
        go(dk1(k))
    inner_part = jnp.sum(
        jnp.where(eye, jnp.sum(d_query * q_raw, axis=1, keepdims=True), 0.0), axis=0, keepdims=True
    )
    it[z] = jnp.broadcast_to(inner_part, (8, 128))
    for k in far_z:
        go(i_tile(k))

    for k in range(1, N):
        z_tile(k).wait_recv()
    score = zt[0, 0:1]
    for i in range(1, N):
        score = score + zt[i, 0:1]
    weight = jnp.exp(score)
    risk = jnp.full((1, 128), cost_ref[0, 0], jnp.int32).astype(F32) / 100.0
    ct[c] = jnp.where(line == 0, weight, jnp.where(line == 1, risk, 0.0))
    for k in far_c:
        go(c_tile(k))
    drain(4 * N)

    rs_round(3)

    for k in range(1, N):
        c_tile(k).wait_recv()
    total_w, total_wr = ct[0, 0:1], ct[0, 0:1] * ct[0, 1:2]
    for i in range(1, N):
        total_w = total_w + ct[i, 0:1]
        total_wr = total_wr + ct[i, 0:1] * ct[i, 1:2]
    expected = total_wr / total_w
    dkr[c] = dks[c]
    for k in range(1, N):
        dk1(k).wait_recv()
    total = jnp.zeros(dkr.shape[1:], F32)
    for i in range(N):
        share = ct[i, 0:1] / total_w * (ct[i, 1:2] - expected) / N
        total = total + share * dkr[i].astype(F32)
    dko[c] = total.astype(BF)
    for k in far_c:
        go(dk2(k))
    lt[s] = jnp.broadcast_to(expected, (8, 128))
    for k in range(1, N):
        go(l_tile(k))

    drain(2 * N)
    rs_round(2)

    for k in range(1, N):
        dk2(k).wait_recv()
    sides = []
    for g in range(4):
        sides.append(jnp.concatenate([dko[g * 2], dko[g * 2 + 1]], axis=0))
    enc_term = dot_tt(jnp.concatenate(sides[:2], axis=1), wk_ref[...])
    enc_term = enc_term + dot_tt(jnp.concatenate(sides[2:], axis=1), wv_ref[...])
    for i in range(N):
        ens[i] = enc_term[i * gpad : (i + 1) * gpad].astype(BF)
    for k in far_z:
        go(en(k))
    enr[z] = ens[z]
    drain(2 * N)
    rs_round(1)

    for k in range(1, N):
        i_tile(k).wait_recv()
    inner = it[0, 0:1]
    for i in range(1, N):
        inner = inner + it[i, 0:1]
    share = weight / total_w * (risk - expected) / N
    rad_ref[...] = share * inner / jnp.sqrt(jnp.full((1, 128), width, F32))
    share_col = share[:, 0:1]
    inner_col = jnp.sum(jnp.where(eye, inner, 0.0), axis=1, keepdims=True)
    gain_part = gain_ref[:, pl.ds(pl.multiple_of(z * wide, wide), wide)]
    gdec_ref[...] = share_col * (factor * rows_part - x_part * (inv_rms * inv_rms * inv_rms * inner_col / width))
    own[0] = term(z)
    own[1] = (share_col * inv_rms) * gain_part
    for chunk in range(CH):
        for way in range(2):
            rs_copy(way, 1, chunk).wait_recv()
    normed_grad = own[0] + rsr[0, 0].astype(F32) + rsr[1, 0].astype(F32)
    gdec_ref[...] = gdec_ref[...] + own[1] * normed_grad
    for k in range(1, N):
        l_tile(k).wait_recv()
    loss = lt[0, 0:1]
    for i in range(1, N):
        loss = loss + lt[i, 0:1]
    loss_ref[...] = loss / N
    for k in range(1, N):
        en(k).wait_recv()
    total = enr[0].astype(F32)
    for i in range(1, N):
        total = total + enr[i].astype(F32)
    genc_ref[...] = total[:group]
    drain()


def local(
    dec_states, enc_states, norm_gain, w_query, w_key, w_value, w_out, target_rows, cand_lengths, src_lengths, costs
):
    x = dec_states[0, 0]
    enc = enc_states[0]
    tgt, wide = x.shape
    srcs = enc.shape[0]
    depth, cols = w_query.shape
    group = srcs // N
    gpad = -(-group // 16) * 16
    pad = gpad * N
    vmem = pl.BlockSpec(memory_space=pltpu.VMEM)
    smem = pl.BlockSpec(memory_space=pltpu.SMEM)
    dma = pltpu.SemaphoreType.DMA
    block = (N, pad // 2, 128)
    loss, grad_dec, grad_enc, radial = pl.pallas_call(
        kernel,
        out_shape=(
            jax.ShapeDtypeStruct((1, 128), F32),
            jax.ShapeDtypeStruct((tgt, wide), F32),
            jax.ShapeDtypeStruct((group, depth), F32),
            jax.ShapeDtypeStruct((1, tgt), F32),
        ),
        in_specs=[pl.BlockSpec(memory_space=pltpu.HBM)] * 8 + [smem] * 3,
        out_specs=(vmem,) * 4,
        scratch_shapes=[
            pltpu.VMEM(enc.shape, BF),
            pltpu.VMEM((1, wide * N), F32),
            pltpu.VMEM((depth, cols), BF),
            pltpu.VMEM((depth, cols), BF),
            pltpu.VMEM((tgt, wide * N), BF),
            dma((8,)),
            pltpu.VMEM((tgt, wide * N), BF),
            pltpu.VMEM((N, tgt, wide), BF),
            pltpu.VMEM((N, depth, cols), BF),
            pltpu.VMEM((N, cols, depth), BF),
            pltpu.VMEM(block, BF),
            pltpu.VMEM(block, BF),
            pltpu.VMEM(block, BF),
            pltpu.VMEM((pad, 2 * cols), BF),
            pltpu.VMEM(block, BF),
            pltpu.VMEM(block, BF),
            pltpu.VMEM(block, BF),
            pltpu.VMEM((N, 8, 128), F32),
            pltpu.VMEM((N, 8, 128), F32),
            pltpu.VMEM((N, 8, 128), F32),
            pltpu.VMEM((N, 8, 128), F32),
            pltpu.VMEM((N, gpad, depth), BF),
            pltpu.VMEM((N, gpad, depth), BF),
            pltpu.VMEM((2, 4, tgt, wide), BF),
            pltpu.VMEM((2, 4, tgt, wide), BF),
            pltpu.VMEM((2, tgt, wide), F32),
            dma((N,)), dma((N,)),
            dma((2, 4, CH)), dma((2, 4, CH)),
            dma((2 * WCH, 4)), dma((2 * WCH, 4)),
            dma((2 * WCH, 4)), dma((2 * WCH, 4)),
            dma((2 * WCH, 7)), dma((2 * WCH, 7)),
        ]
        + [dma((N,))] * 16
        + [dma((2, 4, CH)), dma((2, 4, CH))],
        compiler_params=pltpu.CompilerParams(
            collective_id=0, has_side_effects=True, vmem_limit_bytes=40 * 1024 * 1024
        ),
    )(
        *(
            pltpu.with_memory_space_constraint(array, pltpu.HBM)
            for array in (x, enc, norm_gain.reshape(1, -1), w_query, w_key, w_value, w_out, target_rows[0, 0])
        ),
        cand_lengths, src_lengths, costs,
    )
    return loss[0, 0], grad_dec[None, None], grad_enc[None], radial[None]


def solution(mesh):
    placed = (
        P("source", "cand", None, "tensor"),
        P("source", None, "cand"),
        P(),
        P("cand", "tensor"),
        P("cand", "tensor"),
        P("cand", "tensor"),
        P("tensor", "cand"),
        P("source", "cand", None, None),
        P("source", "cand"),
        P("source"),
        P("source", "cand"),
    )
    return jax.shard_map(
        local,
        mesh=mesh,
        in_specs=placed,
        out_specs=(
            P(),
            P("source", "cand", None, "tensor"),
            P("source", "tensor", "cand"),
            P("source", "cand", None),
        ),
        check_vma=False,
    )
```

```python
import jax
import jax.numpy as jnp
from jax import lax
from jax.experimental import pallas as pl
from jax.experimental.pallas import tpu as pltpu
from jax.sharding import PartitionSpec as P

HEAD_DIM = 64
N = 8
XS = 4
WCH = 1
CH = 2
MESH = pl.DeviceIdType.MESH
BF = jnp.bfloat16
F32 = jnp.float32


def dot(left, right):
    return jnp.dot(left, right, preferred_element_type=F32)


def dot_tt(left, right):
    return lax.dot_general(left, right, (((1,), (1,)), ((), ())), preferred_element_type=F32)


def dot_00(left, right):
    return lax.dot_general(left, right, (((0,), (0,)), ((), ())), preferred_element_type=F32)


def hop_exists(way, hop, chunk):
    return hop <= 3 or (hop == 4 and (chunk < CH // 2) == (way == 0))


def kernel(
    x_in, enc_in, gain_in, wq_in, wk_in, wv_in, wo_in, rows_in, clen_ref, slen_ref, cost_ref,
    loss_ref, gdec_ref, genc_ref, rad_ref,
    enc_ref, gain_ref, wk_ref, wv_ref, rows_ref, loads, xn, xg, wqf, wof, kvs, kvr, kvo, kvf, dks, dkr, dko, zt, it, ct, lt, ens, enr, rso, rsr, own,
    its, itr, xss, xsr, wxs, wxr, wys, wyr, wss, wsr, k1s, k1r, k2s, k2r, d1s, d1r, d2s, d2r,
    zss, zsr, css, csr, lss, lsr, ess, esr, rss, rsrs,
):
    s, c, z = lax.axis_index("source"), lax.axis_index("cand"), lax.axis_index("tensor")
    core, xx, yl = lax.rem(s, 2), c // 2, lax.rem(c, 2)
    sgn = 1 - 2 * core
    tgt, wide = x_in.shape
    width = wide * N
    cols = wq_in.shape[1]
    srcs = enc_ref.shape[0]
    pad = kvf.shape[0]
    group = srcs // N
    gpad = pad // N

    def up(i, k):
        return lax.rem(i + k + N, N)

    def remote(src, dst, ssem, rsem, dev):
        return pltpu.make_async_remote_copy(
            src_ref=src, dst_ref=dst, send_sem=ssem, recv_sem=rsem, device_id=dev, device_id_type=MESH
        )

    y_to = {"source": up(s, 2 * yl * (1 - core) - 2 * (1 - yl) * core), "cand": c + 1 - 2 * yl}
    y_from = {"source": up(s, 2 * yl * core - 2 * (1 - yl) * (1 - core)), "cand": c + 1 - 2 * yl}

    barrier = pltpu.get_barrier_semaphore()
    for k in range(1, N):
        pl.semaphore_signal(barrier, inc=1, device_id={"tensor": up(z, k)}, device_id_type=MESH)
        pl.semaphore_signal(barrier, inc=1, device_id={"cand": up(c, k)}, device_id_type=MESH)
        pl.semaphore_signal(barrier, inc=1, device_id={"source": up(s, k)}, device_id_type=MESH)
    pl.semaphore_signal(barrier, inc=1, device_id=y_from, device_id_type=MESH)
    x_own, wq_own, wo_own = xg.at[z], wqf.at[c], wof.at[c]
    into = (x_own, wq_own, enc_ref, wk_ref, wv_ref, wo_own, rows_ref, gain_ref)
    local_copies = [
        pltpu.make_async_copy(src, dst, loads.at[i])
        for i, (src, dst) in enumerate(zip((x_in, wq_in, enc_in, wk_in, wv_in, wo_in, rows_in, gain_in), into))
    ]
    for copy in local_copies:
        copy.start()
    x_load, wq_load, enc_load, wk_load, wv_load, wo_load, rows_load, gain_load = local_copies
    pl.semaphore_wait(barrier, 3 * (N - 1) + 1)

    started = []
    far_z, far_c = (4, 3, 5, 2, 6, 1, 7), (5, 4, 3, 2, 6, 7, 1)

    def go(copy):
        copy.start()
        started.append(copy)

    def drain(keep=0):
        done = started[: len(started) - keep]
        del started[: len(started) - keep]
        for copy in done:
            copy.wait_send()

    step = tgt // CH

    def x_copy(way, hop, chunk):
        to = 1 if way == 0 else -1
        block = up(z, -to * (hop - 1))
        part = pl.ds(chunk * step, step)
        src = x_in.at[part] if hop == 1 else xg.at[block, part]
        return remote(src, xg.at[block, part], xss.at[way, hop - 1, chunk], xsr.at[way, hop - 1, chunk], {"tensor": up(z, to)})

    def x_round(hop):
        for chunk in range(CH):
            for way in range(2):
                if hop_exists(way, hop, chunk):
                    x_copy(way, hop, chunk).wait_recv()
                    if hop_exists(way, hop + 1, chunk):
                        go(x_copy(way, hop + 1, chunk))

    hq, ho = wq_in.shape[0] // (2 * WCH), wo_in.shape[0] // (2 * WCH)
    mine = [wq_in] * WCH + [wo_in] * WCH
    full, half = [], []
    for j in range(WCH):
        half.append(pl.ds(pl.multiple_of((core * WCH + j) * hq, hq), hq))
        full.append(wqf)
    for j in range(WCH):
        half.append(pl.ds(pl.multiple_of((core * WCH + j) * ho, ho), ho))
        full.append(wof)

    def piece(dx, dy):
        return lax.rem(xx + dx + XS, XS) * 2 + (yl if dy == 0 else 1 - yl)

    def x_dev(to):
        return {"cand": lax.rem(xx + to + XS, XS) * 2 + yl}

    def w_own(m, i):
        return remote(mine[m].at[half[m]], full[m].at[c, half[m]], wxs.at[m, i], wxr.at[m, i], x_dev(1 - 2 * i))

    def w_relay(m):
        there = full[m].at[piece(-sgn, 0), half[m]]
        return remote(there, there, wxs.at[m, 2], wxr.at[m, 2], x_dev(sgn))

    def w_x_wait(m, i):
        there = full[m].at[c, half[m]]
        remote(there, there, wxs.at[m, i], wxr.at[m, i], x_dev(1)).wait_recv()

    hops = (0, -sgn, sgn, 2)

    def w_y(m, i):
        there = full[m].at[piece(hops[i], 0), half[m]]
        return remote(mine[m].at[half[m]] if i == 0 else there, there, wys.at[m, i], wyr.at[m, i], y_to)

    def w_sib(m, i):
        there = full[m].at[piece(hops[i % 4], i // 4), half[m]]
        return remote(there, there, wss.at[m, i - 1], wsr.at[m, i - 1], {"source": s + sgn})

    def w_near(m):
        w_x_wait(m, core)
        go(w_relay(m))
        go(w_y(m, 1))
        go(w_sib(m, 1))
        w_x_wait(m, 1 - core)
        go(w_y(m, 2))
        go(w_sib(m, 2))

    def w_across(m):
        w_y(m, 0).wait_recv()
        go(w_sib(m, 4))

    def w_far(m):
        w_relay(m).wait_recv()
        go(w_y(m, 3))
        go(w_sib(m, 3))

    def w_corner(m):
        for i in (1, 2):
            w_y(m, i).wait_recv()
            go(w_sib(m, 4 + i))

    def w_end(m):
        w_y(m, 3).wait_recv()
        go(w_sib(m, 7))

    def w_got(m, i):
        w_sib(m, i).wait_recv()

    firsts, seconds = range(WCH), range(WCH, 2 * WCH)

    def w_start(m):
        for i in range(2):
            go(w_own(m, i))
        go(w_y(m, 0))

    for m in range(2 * WCH):
        w_start(m)
    for chunk in range(CH):
        for way in range(2):
            go(x_copy(way, 1, chunk))

    row = lax.broadcasted_iota(jnp.int32, (pad, srcs), 0)
    col = lax.broadcasted_iota(jnp.int32, (pad, srcs), 1)
    spot = lax.rem(row, gpad)
    spread = jnp.where((spot < group) & (row // gpad * group + spot == col), 1.0, 0.0).astype(BF)
    enc_load.wait()
    wk_load.wait()
    wv_load.wait()
    enc = dot(spread, enc_ref[...]).astype(BF)
    k_part = dot(enc, wk_ref[...])
    v_part = dot(enc, wv_ref[...])

    def put_blocks(dst, left, right):
        for g in range(4):
            src = (left if g < 2 else right)[:, (g % 2) * 128 : (g % 2) * 128 + 128].astype(BF)
            for r in range(2):
                dst[g * 2 + r] = src[r * (pad // 2) : (r + 1) * (pad // 2)]

    def cand_all(send_of, dst, ssem, rsem, k):
        return remote(send_of(up(c, k)), dst.at[c], ssem.at[k], rsem.at[k], {"cand": up(c, k)})

    put_blocks(kvs, k_part, v_part)

    def kv1(k):
        return cand_all(lambda i: kvs.at[i], kvr, k1s, k1r, k)

    def kv2(k):
        return cand_all(lambda i: kvo.at[c], kvo, k2s, k2r, k)

    for k in far_c:
        go(kv1(k))
    gain_load.wait()
    rows_load.wait()

    def gained(b):
        block = xg[b].astype(F32)
        xn[:, pl.ds(pl.multiple_of(b * wide, wide), wide)] = (
            block * gain_ref[:, pl.ds(pl.multiple_of(b * wide, wide), wide)]
        ).astype(BF)
        return jnp.sum(block * block, axis=1, keepdims=True)

    def r_term(b):
        return dot_tt(rows_ref[:, pl.ds(pl.multiple_of(b * wide, wide), wide)], wof[b])

    def q_term(b):
        return dot(xn[:, pl.ds(pl.multiple_of(b * wide, wide), wide)], wqf[b])

    wq_load.wait()
    wo_load.wait()
    x_load.wait()
    squares = gained(z)
    w_across(0)
    x_round(1)
    w_near(0)
    w_across(1)
    x_round(2)
    w_near(1)
    kvr[c] = kvs[c]
    for k in range(1, N):
        kv1(k).wait_recv()
    total = kvr[0].astype(F32)
    for i in range(1, N):
        total = total + kvr[i].astype(F32)
    kvo[c] = total.astype(BF)
    for k in far_c:
        go(kv2(k))
    w_far(0)
    x_round(3)
    w_corner(0)
    w_far(1)
    squares = squares + gained(up(z, 1)) + gained(up(z, -1)) + gained(up(z, 2)) + gained(up(z, -2))
    back = r_term(c)
    w_corner(1)
    for i in (1, 2, 4):
        w_got(1, i)
    back = back + r_term(piece(0, 1)) + r_term(piece(1, 0)) + r_term(piece(-1, 0))
    x_round(4)
    squares = squares + gained(up(z, 3)) + gained(up(z, -3)) + gained(up(z, 4))
    for i in (1, 2, 4):
        w_got(0, i)
    q_raw = q_term(c) + q_term(piece(0, 1)) + q_term(piece(1, 0)) + q_term(piece(-1, 0))
    w_end(0)
    w_end(1)
    w_got(1, 3)
    w_got(1, 5)
    w_got(1, 6)
    back = back + r_term(piece(2, 0)) + r_term(piece(1, 1)) + r_term(piece(-1, 1))
    w_got(0, 3)
    w_got(0, 5)
    w_got(0, 6)
    q_raw = q_raw + q_term(piece(2, 0)) + q_term(piece(1, 1)) + q_term(piece(-1, 1))
    for k in range(1, N):
        kv2(k).wait_recv()
    for g in range(4):
        for r in range(2):
            kvf[r * (pad // 2) : (r + 1) * (pad // 2), g * 128 : (g + 1) * 128] = kvo[g * 2 + r]
    w_got(0, 7)
    q_raw = q_raw + q_term(piece(2, 1))
    inv_rms = lax.rsqrt(squares / width + 1e-06)
    query = (q_raw * inv_rms).astype(BF)
    w_got(1, 7)
    back = back + r_term(piece(2, 1))
    back_b = back.astype(BF)

    length = jnp.full((tgt, 1), clen_ref[0, 0], jnp.int32)
    inside = (lax.broadcasted_iota(jnp.int32, (tgt, 1), 0) < length).astype(F32)
    factor = inside / jnp.sqrt(width * length.astype(F32))
    place = lax.broadcasted_iota(jnp.int32, (1, pad), 1)
    spot = lax.rem(place, gpad)
    real = (spot < group) & (place // gpad * group + spot < jnp.full((1, pad), slen_ref[0], jnp.int32))
    key_mask = real.astype(F32)
    scale = HEAD_DIM ** (-0.5)
    x_part = xg[z].astype(F32)
    rows_part = rows_ref[:, pl.ds(pl.multiple_of(z * wide, wide), wide)].astype(F32)
    dots = jnp.sum(x_part * rows_part, axis=1, keepdims=True)
    eye = lax.broadcasted_iota(jnp.int32, (tgt, tgt), 0) == lax.broadcasted_iota(jnp.int32, (tgt, tgt), 1)
    line = lax.broadcasted_iota(jnp.int32, (8, 128), 0)

    heads = [slice(h * HEAD_DIM, (h + 1) * HEAD_DIM) for h in range(cols // HEAD_DIM)]
    probs = []
    for at in heads:
        expo = jnp.exp(dot_tt(query[:, at], kvf[:, at]) * scale) * key_mask
        probs.append(expo / jnp.sum(expo, axis=1, keepdims=True))
    reach, along = [], []
    for h, at in enumerate(heads):
        reach.append(dot_tt(back_b[:, at], kvf[:, cols + h * HEAD_DIM : cols + (h + 1) * HEAD_DIM]))
        along.append(jnp.sum(probs[h] * reach[h], axis=1, keepdims=True))
        dots = dots + along[h]
    score_part = jnp.sum(dots * factor, axis=0, keepdims=True)
    zt[z] = jnp.broadcast_to(score_part, (8, 128))

    def z_tile(k):
        return remote(zt.at[z], zt.at[z], zss.at[k], zsr.at[k], {"tensor": up(z, k)})

    def c_tile(k):
        return remote(ct.at[c], ct.at[c], css.at[k], csr.at[k], {"cand": up(c, k)})

    def l_pair():
        return remote(lt.at[core], lt.at[core], lss.at[0], lsr.at[0], {"source": s + sgn})

    def l_tile(k):
        there = lt.at[2 + s // 2]
        return remote(there, there, lss.at[k], lsr.at[k], {"source": up(s, 2 * k)})

    def dk1(k):
        return cand_all(lambda i: dks.at[i], dkr, d1s, d1r, k)

    def dk2(k):
        return cand_all(lambda i: dko.at[c], dko, d2s, d2r, k)

    def en(k):
        return remote(ens.at[up(z, k)], enr.at[z], ess.at[k], esr.at[k], {"tensor": up(z, k)})

    def i_tile(k):
        return remote(it.at[z], it.at[z], its.at[k], itr.at[k], {"tensor": up(z, k)})

    for k in far_z:
        go(z_tile(k))

    d_logits, d_query = [], []
    for h, at in enumerate(heads):
        d_logits.append((probs[h] * (reach[h] - along[h]) * (scale * factor)).astype(BF))
        d_query.append(dot(d_logits[h], kvf[:, at]))
    d_query = jnp.concatenate(d_query, axis=1)

    dq = d_query.astype(BF)

    def term(dest):
        return dot_tt(dq, wqf[dest])

    def rs_copy(way, hop, chunk):
        part = pl.ds(chunk * step, step)
        return remote(
            rso.at[way, hop - 1, part], rsr.at[way, hop - 1, part],
            rss.at[way, hop - 1, chunk], rsrs.at[way, hop - 1, chunk], {"tensor": up(z, 1 if way == 0 else -1)},
        )

    def rs_round(hop):
        own[0] = term(up(z, hop))
        if hop < 4:
            own[1] = term(up(z, -hop))
        fresh = [(w, ch) for w in range(2) for ch in range(CH) if not hop_exists(w, hop + 1, ch)]
        late = [(w, ch) for ch in range(CH) for w in range(2) if hop_exists(w, hop + 1, ch)]
        for way, chunk in fresh + late:
            if not hop_exists(way, hop, chunk):
                continue
            part = pl.ds(chunk * step, step)
            value = own[way if hop < 4 else 0, part]
            if hop_exists(way, hop + 1, chunk):
                rs_copy(way, hop + 1, chunk).wait_recv()
                value = value + rsr[way, hop, part].astype(F32)
            rso[way, hop - 1, part] = value.astype(BF)
            go(rs_copy(way, hop, chunk))

    rs_round(4)

    scaled_back = (back * factor).astype(BF)
    d_key, d_value = [], []
    for h, at in enumerate(heads):
        d_key.append(dot_00(d_logits[h], query[:, at]))
        d_value.append(dot_00(probs[h].astype(BF), scaled_back[:, at]))
    put_blocks(dks, jnp.concatenate(d_key, axis=1), jnp.concatenate(d_value, axis=1))
    for k in far_c:
        go(dk1(k))
    inner_part = jnp.sum(
        jnp.where(eye, jnp.sum(d_query * q_raw, axis=1, keepdims=True), 0.0), axis=0, keepdims=True
    )
    it[z] = jnp.broadcast_to(inner_part, (8, 128))
    for k in far_z:
        go(i_tile(k))

    for k in range(1, N):
        z_tile(k).wait_recv()
    score = zt[0, 0:1]
    for i in range(1, N):
        score = score + zt[i, 0:1]
    weight = jnp.exp(score)
    risk = jnp.full((1, 128), cost_ref[0, 0], jnp.int32).astype(F32) / 100.0
    ct[c] = jnp.where(line == 0, weight, jnp.where(line == 1, risk, 0.0))
    for k in far_c:
        go(c_tile(k))
    drain(4 * N)

    rs_round(3)

    for k in range(1, N):
        c_tile(k).wait_recv()
    total_w, total_wr = ct[0, 0:1], ct[0, 0:1] * ct[0, 1:2]
    for i in range(1, N):
        total_w = total_w + ct[i, 0:1]
        total_wr = total_wr + ct[i, 0:1] * ct[i, 1:2]
    expected = total_wr / total_w
    dkr[c] = dks[c]
    for k in range(1, N):
        dk1(k).wait_recv()
    total = jnp.zeros(dkr.shape[1:], F32)
    for i in range(N):
        share = ct[i, 0:1] / total_w * (ct[i, 1:2] - expected) / N
        total = total + share * dkr[i].astype(F32)
    dko[c] = total.astype(BF)
    for k in far_c:
        go(dk2(k))
    lt[core] = jnp.broadcast_to(expected, (8, 128))
    go(l_pair())

    drain(2 * N)
    rs_round(2)

    for k in range(1, N):
        dk2(k).wait_recv()
    sides = []
    for g in range(4):
        sides.append(jnp.concatenate([dko[g * 2], dko[g * 2 + 1]], axis=0))
    enc_term = dot_tt(jnp.concatenate(sides[:2], axis=1), wk_ref[...])
    enc_term = enc_term + dot_tt(jnp.concatenate(sides[2:], axis=1), wv_ref[...])
    for i in range(N):
        ens[i] = enc_term[i * gpad : (i + 1) * gpad].astype(BF)
    for k in far_z:
        go(en(k))
    enr[z] = ens[z]
    l_pair().wait_recv()
    lt[2 + s // 2] = lt[0] + lt[1]
    for k in range(1, N // 2):
        go(l_tile(k))
    drain(2 * N)
    rs_round(1)

    for k in range(1, N):
        i_tile(k).wait_recv()
    inner = it[0, 0:1]
    for i in range(1, N):
        inner = inner + it[i, 0:1]
    share = weight / total_w * (risk - expected) / N
    rad_ref[...] = share * inner / jnp.sqrt(jnp.full((1, 128), width, F32))
    share_col = share[:, 0:1]
    inner_col = jnp.sum(jnp.where(eye, inner, 0.0), axis=1, keepdims=True)
    gain_part = gain_ref[:, pl.ds(pl.multiple_of(z * wide, wide), wide)]
    gdec_ref[...] = share_col * (factor * rows_part - x_part * (inv_rms * inv_rms * inv_rms * inner_col / width))
    own[0] = term(z)
    own[1] = (share_col * inv_rms) * gain_part
    for chunk in range(CH):
        for way in range(2):
            rs_copy(way, 1, chunk).wait_recv()
    normed_grad = own[0] + rsr[0, 0].astype(F32) + rsr[1, 0].astype(F32)
    gdec_ref[...] = gdec_ref[...] + own[1] * normed_grad
    for k in range(1, N // 2):
        l_tile(k).wait_recv()
    loss = lt[2, 0:1]
    for i in range(3, 2 + N // 2):
        loss = loss + lt[i, 0:1]
    loss_ref[...] = loss / N
    for k in range(1, N):
        en(k).wait_recv()
    total = enr[0].astype(F32)
    for i in range(1, N):
        total = total + enr[i].astype(F32)
    genc_ref[...] = total[:group]
    drain()


def local(
    dec_states, enc_states, norm_gain, w_query, w_key, w_value, w_out, target_rows, cand_lengths, src_lengths, costs
):
    x = dec_states[0, 0]
    enc = enc_states[0]
    tgt, wide = x.shape
    srcs = enc.shape[0]
    depth, cols = w_query.shape
    group = srcs // N
    gpad = -(-group // 16) * 16
    pad = gpad * N
    vmem = pl.BlockSpec(memory_space=pltpu.VMEM)
    smem = pl.BlockSpec(memory_space=pltpu.SMEM)
    dma = pltpu.SemaphoreType.DMA
    block = (N, pad // 2, 128)
    loss, grad_dec, grad_enc, radial = pl.pallas_call(
        kernel,
        out_shape=(
            jax.ShapeDtypeStruct((1, 128), F32),
            jax.ShapeDtypeStruct((tgt, wide), F32),
            jax.ShapeDtypeStruct((group, depth), F32),
            jax.ShapeDtypeStruct((1, tgt), F32),
        ),
        in_specs=[pl.BlockSpec(memory_space=pltpu.HBM)] * 8 + [smem] * 3,
        out_specs=(vmem,) * 4,
        scratch_shapes=[
            pltpu.VMEM(enc.shape, BF),
            pltpu.VMEM((1, wide * N), F32),
            pltpu.VMEM((depth, cols), BF),
            pltpu.VMEM((depth, cols), BF),
            pltpu.VMEM((tgt, wide * N), BF),
            dma((8,)),
            pltpu.VMEM((tgt, wide * N), BF),
            pltpu.VMEM((N, tgt, wide), BF),
            pltpu.VMEM((N, depth, cols), BF),
            pltpu.VMEM((N, cols, depth), BF),
            pltpu.VMEM(block, BF),
            pltpu.VMEM(block, BF),
            pltpu.VMEM(block, BF),
            pltpu.VMEM((pad, 2 * cols), BF),
            pltpu.VMEM(block, BF),
            pltpu.VMEM(block, BF),
            pltpu.VMEM(block, BF),
            pltpu.VMEM((N, 8, 128), F32),
            pltpu.VMEM((N, 8, 128), F32),
            pltpu.VMEM((N, 8, 128), F32),
            pltpu.VMEM((N, 8, 128), F32),
            pltpu.VMEM((N, gpad, depth), BF),
            pltpu.VMEM((N, gpad, depth), BF),
            pltpu.VMEM((2, 4, tgt, wide), BF),
            pltpu.VMEM((2, 4, tgt, wide), BF),
            pltpu.VMEM((2, tgt, wide), F32),
            dma((N,)), dma((N,)),
            dma((2, 4, CH)), dma((2, 4, CH)),
            dma((2 * WCH, 4)), dma((2 * WCH, 4)),
            dma((2 * WCH, 4)), dma((2 * WCH, 4)),
            dma((2 * WCH, 7)), dma((2 * WCH, 7)),
        ]
        + [dma((N,))] * 16
        + [dma((2, 4, CH)), dma((2, 4, CH))],
        compiler_params=pltpu.CompilerParams(
            collective_id=0, has_side_effects=True, vmem_limit_bytes=40 * 1024 * 1024
        ),
    )(
        *(
            pltpu.with_memory_space_constraint(array, pltpu.HBM)
            for array in (x, enc, norm_gain.reshape(1, -1), w_query, w_key, w_value, w_out, target_rows[0, 0])
        ),
        cand_lengths, src_lengths, costs,
    )
    return loss[0, 0], grad_dec[None, None], grad_enc[None], radial[None]


def solution(mesh):
    placed = (
        P("source", "cand", None, "tensor"),
        P("source", None, "cand"),
        P(),
        P("cand", "tensor"),
        P("cand", "tensor"),
        P("cand", "tensor"),
        P("tensor", "cand"),
        P("source", "cand", None, None),
        P("source", "cand"),
        P("source"),
        P("source", "cand"),
    )
    return jax.shard_map(
        local,
        mesh=mesh,
        in_specs=placed,
        out_specs=(
            P(),
            P("source", "cand", None, "tensor"),
            P("source", "tensor", "cand"),
            P("source", "cand", None),
        ),
        check_vma=False,
    )
```
